128 devices in a mesh: dp: 32 (over y, x_hi, z), mp: 4 (over x_lo, core).
Axes of the slice: x: 4 (x_hi: 2, x_lo: 2; x = x_hi * 2 + x_lo), y: 4, z: 4, core: 2. Of those that a mesh axis runs over, the one named last changes fastest.
Arguments:
- passages: bfloat16 [256, 128, 4096], P('dp'), may hold values from -6 to 6
- lengths: int32 [256], P('dp'), may hold values from 16 to 128, as said below
- owner: int32 [256], P('dp'), may hold values from 0 to 31, as said below
- enc_gain: float32 [4096], replicated, may hold values from 0.25 to 2.5
- final_gain: float32 [4096], replicated, may hold values from 0.25 to 2.5
- enc_wq: bfloat16 [4096, 2048], P('dp', 'mp'), may hold values from -2 to 2
- enc_wk: bfloat16 [4096, 2048], P('dp', 'mp'), may hold values from -0.09375 to 0.09375
- enc_wv: bfloat16 [4096, 2048], P('dp', 'mp'), may hold values from -0.09375 to 0.09375
- enc_wo: bfloat16 [2048, 4096], P('mp', 'dp'), may hold values from -0.125 to 0.125
- dec_wk: bfloat16 [4096, 2048], P('dp', 'mp'), may hold values from -0.09375 to 0.09375
- dec_wv: bfloat16 [4096, 2048], P('dp', 'mp'), may hold values from -0.09375 to 0.09375
- dec_query: bfloat16 [32, 32, 2048], P(None, None, 'mp'), may hold values from -3 to 3
Outputs:
- encoded: bfloat16 [256, 128, 4096], P('dp')
- context: bfloat16 [32, 32, 2048], P('dp', None, 'mp')
The draws below stay inside these ranges and needn't reach their ends.
Inputs may be any that keep to these rules, and one draw needn't show every extreme that they name: `lengths`: every device's first passage has length 128. `owner`: each question owns exactly 8 passages, spread over the devices at random.
All inputs are finite; a program needn't handle non-finite values.
Results may differ from the reference program's by a relative error of at most 0.038.
Values may be sent and summed in bfloat16 or wider, within the bound.
No kernel may reach another device: no remote copies, remote signals or barrier semaphores. Data moves between devices by JAX's collectives and lax.ppermute only.
A program may use at most 128 MiB of HBM per device.

```python
import math
import jax
import jax.numpy as jnp
from jax import lax

D = 4096
HEADS = 32
HD = 64
L = 128
NP = 8
DEC = 32
PASS_DEV = 8
QUESTIONS = 32
PASSAGES = 256
GROUP_HEADS = 8
N_DP = 32


def draw_lengths(key, part):
    key = jax.random.fold_in(key, 1)
    drawn = jax.random.randint(key, (PASSAGES,), max(1, L // 8), L + 1, dtype=jnp.int32)
    drawn = drawn.reshape(N_DP, PASS_DEV).at[:, 0].set(L)
    return drawn.reshape(PASSAGES).astype(jnp.int32)


def draw_owner(key, part):
    key = jax.random.fold_in(key, 2)
    shuffled = jax.random.permutation(key, PASSAGES).astype(jnp.int32)
    return (shuffled // NP).astype(jnp.int32)


def draw_enc_wq(key, part):
    key = jax.random.fold_in(key, 3)
    spread = 11.0 / HD ** 0.5 / D ** 0.5
    values = jnp.clip(jax.random.normal(key, (D, HEADS * HD), jnp.float32), -4.0, 4.0) * spread
    return values.astype(jnp.bfloat16)


def block_levels(rng, shape, pieces, low, high):
    factor_of = 1.0
    for dim, parts in pieces:
        steps = jax.random.uniform(jax.random.fold_in(jax.random.fold_in(rng, 6), dim), (parts,), jnp.float32, low / len(pieces), high / len(pieces))
        factor_of = factor_of * jnp.repeat(jnp.exp(steps), shape[dim] // parts).reshape((-1,) + (1,) * (len(shape) - 1 - dim))
    return factor_of


def scatter_about(rng, shape, width, limit, pieces=(), kind=jnp.bfloat16):
    values = width * jax.random.normal(rng, shape, jnp.float32)
    if pieces:
        values = values * block_levels(rng, shape, pieces, -0.22, 0.18)
    return jnp.clip(values, -limit, limit).astype(kind)


def setup_inputs(seed: int = 0) -> dict:
    key_of = jax.random.split(jax.random.key(seed), 13)
    passages = scatter_about(key_of[0], (PASSAGES, L, D), 1.0, 6.0, ((0, 32),))
    lengths = draw_lengths(jax.random.fold_in(key_of[12], 71), 0)
    owner = draw_owner(jax.random.fold_in(key_of[12], 71), 0)
    enc_gain = jnp.clip(jnp.exp(jax.random.uniform(key_of[3], (D,), jnp.float32, math.log(0.25), math.log(2.5))), 0.25, 2.5)
    final_gain = jnp.clip(jnp.exp(jax.random.uniform(key_of[4], (D,), jnp.float32, math.log(0.25), math.log(2.5))), 0.25, 2.5)
    enc_wq = draw_enc_wq(jax.random.fold_in(key_of[12], 71), 0)
    enc_wk = scatter_about(key_of[6], (D, HEADS * HD), D ** -0.5, 0.09375, ((0, 32), (1, 4)))
    enc_wv = scatter_about(key_of[7], (D, HEADS * HD), D ** -0.5, 0.09375, ((0, 32), (1, 4)))
    enc_wo = scatter_about(key_of[8], (HEADS * HD, D), (HEADS * HD) ** -0.5, 0.125, ((0, 4), (1, 32)))
    dec_wk = scatter_about(key_of[9], (D, HEADS * HD), D ** -0.5, 0.09375, ((0, 32), (1, 4)))
    dec_wv = scatter_about(key_of[10], (D, HEADS * HD), D ** -0.5, 0.09375, ((0, 32), (1, 4)))
    dec_query = scatter_about(key_of[11], (QUESTIONS, DEC, HEADS * HD), 1.0, 3.0, ((2, 4),))
    return {"passages": passages, "lengths": lengths, "owner": owner, "enc_gain": enc_gain, "final_gain": final_gain, "enc_wq": enc_wq, "enc_wk": enc_wk, "enc_wv": enc_wv, "enc_wo": enc_wo, "dec_wk": dec_wk, "dec_wv": dec_wv, "dec_query": dec_query}


EPS = 1e-06
SCALE = 0.125

def rms_norm(values, gain_vec):
    return values * lax.rsqrt(lax.optimization_barrier(jnp.mean(values * values, axis=-1, keepdims=True)) + EPS) * gain_vec

def round_half(values):
    return lax.optimization_barrier(values.astype(jnp.bfloat16)).astype(jnp.float32)

def reference(passages, lengths, owner, enc_gain, final_gain, enc_wq, enc_wk, enc_wv, enc_wo, dec_wk, dec_wv, dec_query):
    group_count = HEADS // GROUP_HEADS
    wo_groups = enc_wo.reshape(group_count, GROUP_HEADS * HD, D).astype(jnp.float32)

    def encode_one(inputs):
        passage, length = inputs
        floats = passage.astype(jnp.float32)
        normed = rms_norm(floats, enc_gain).astype(jnp.bfloat16)
        queries = jnp.dot(normed, enc_wq, preferred_element_type=jnp.float32).astype(jnp.bfloat16).reshape(L, HEADS, HD)
        keys_enc = jnp.dot(normed, enc_wk, preferred_element_type=jnp.float32).astype(jnp.bfloat16).reshape(L, HEADS, HD)
        values_enc = jnp.dot(normed, enc_wv, preferred_element_type=jnp.float32).astype(jnp.bfloat16).reshape(L, HEADS, HD)
        scores = jnp.einsum('qhd,khd->hqk', queries.astype(jnp.float32), keys_enc.astype(jnp.float32)) * SCALE
        visible = jnp.arange(L, dtype=jnp.int32) < length
        expon = jnp.where(visible[None, None, :], jnp.exp(scores), 0.0)
        weights = (expon / lax.optimization_barrier(jnp.sum(expon, axis=-1, keepdims=True))).astype(jnp.bfloat16)
        attended = jnp.einsum('hqk,khd->qhd', weights.astype(jnp.float32), values_enc.astype(jnp.float32)).astype(jnp.bfloat16)
        grouped = attended.reshape(L, group_count, GROUP_HEADS * HD).astype(jnp.float32)
        partial_value = jnp.einsum('lgc,gcd->gld', grouped, wo_groups)
        summed = lax.optimization_barrier(jnp.sum(round_half(partial_value), axis=0))
        encoded = (floats + summed).astype(jnp.bfloat16)
        final = rms_norm(encoded.astype(jnp.float32), final_gain).astype(jnp.bfloat16)
        dkeys = jnp.dot(final, dec_wk, preferred_element_type=jnp.float32).astype(jnp.bfloat16)
        dvalues = jnp.dot(final, dec_wv, preferred_element_type=jnp.float32).astype(jnp.bfloat16)
        return (encoded, dkeys, dvalues)
    encoded, dkeys, dvalues = lax.map(encode_one, (passages, lengths))
    order = jnp.argsort(owner, stable=True).astype(jnp.int32).reshape(QUESTIONS, NP)

    def decode_one(inputs):
        question_query, chosen = inputs
        picked_keys = dkeys[chosen].reshape(NP * L, HEADS, HD).astype(jnp.float32)
        picked_values = dvalues[chosen].reshape(NP * L, HEADS, HD).astype(jnp.float32)
        visible = (jnp.arange(L, dtype=jnp.int32)[None, :] < lengths[chosen][:, None]).reshape(NP * L)
        query = question_query.reshape(DEC, HEADS, HD).astype(jnp.float32)
        scores = jnp.einsum('thd,khd->thk', query, picked_keys) * SCALE
        expon = jnp.where(visible[None, None, :], jnp.exp(scores), 0.0)
        total = lax.optimization_barrier(jnp.sum(expon, axis=-1))
        numer = jnp.einsum('thk,khd->thd', expon, picked_values, precision=lax.Precision.HIGHEST)
        return (numer / total[..., None]).astype(jnp.bfloat16).reshape(DEC, HEADS * HD)
    context = lax.map(decode_one, (dec_query, order))
    return (encoded, context)
```

```python
import jax
import jax.numpy as jnp
from jax import lax
from jax.sharding import Mesh, PartitionSpec as P

HD = 64

EPS = 1e-06
SCALE = 0.125
AXES = ("y", "xh", "z", "xl", "c")
SIZES = (4, 2, 4, 2, 2)
DP = ("y", "xh", "z")
MP = ("xl", "c")


def swap(values, axis):
    return lax.ppermute(values, axis, [(0, 1), (1, 0)])


def in_order(mine, other, axis):
    first = lax.axis_index(axis) == 0
    return jnp.where(first, mine, other), jnp.where(first, other, mine)


def gather_rows(parts):
    count, rows, cols = parts.shape
    lo, hi = in_order(parts, swap(parts, "xh"), "xh")
    both = jnp.stack([lo, hi])
    full = lax.all_gather(both, ("y", "z"), axis=0, tiled=False)
    full = full.reshape(4, 4, 2, count, rows, cols)
    return [full[:, :, :, i].transpose(0, 2, 1, 3, 4).reshape(-1, cols) for i in range(count)]


def shards(
    passages,
    lengths,
    owner,
    enc_gain,
    final_gain,
    enc_wq,
    enc_wk,
    enc_wv,
    enc_wo,
    dec_wk,
    dec_wv,
    dec_query,
):
    pass_count, seq_len, width = passages.shape
    tok_rows = pass_count * seq_len
    local_cols = enc_wq.shape[1]
    local_heads = local_cols // HD
    floats = passages.reshape(tok_rows, width).astype(jnp.float32)

    def rms_norm(values, gain_vec):
        return values * lax.rsqrt(jnp.mean(values * values, axis=-1, keepdims=True) + EPS) * gain_vec

    def mm(a, b):
        return jnp.dot(a, b, preferred_element_type=jnp.float32)

    normed = rms_norm(floats, enc_gain).astype(jnp.bfloat16)
    wq, wk, wv = gather_rows(jnp.stack([enc_wq, enc_wk, enc_wv]))
    wo_lo, wo_hi = in_order(enc_wo, swap(enc_wo, "xl"), "xl")
    wo_both = jnp.concatenate([wo_lo, wo_hi], axis=0)
    wo_x = jnp.stack(in_order(wo_both, swap(wo_both, "xh"), "xh"))
    wo_full = lax.all_gather(wo_x, ("y", "z"), axis=0, tiled=False)
    wo_full = wo_full.reshape(4, 4, 2, 2 * local_cols, -1).transpose(3, 0, 2, 1, 4).reshape(2 * local_cols, width)
    dwk, dwv = gather_rows(jnp.stack([dec_wk, dec_wv]))

    def by_heads(values):
        return values.astype(jnp.bfloat16).reshape(pass_count, seq_len, local_heads, HD)

    queries = by_heads(mm(normed, wq))
    keys_enc = by_heads(mm(normed, wk))
    values_enc = by_heads(mm(normed, wv))
    visible = lax.broadcasted_iota(jnp.int32, (pass_count, seq_len), 1) < lengths[:, None]
    scores = jnp.einsum("pqhd,pkhd->phqk", queries, keys_enc, preferred_element_type=jnp.float32) * SCALE
    expon = jnp.where(visible[:, None, None, :], jnp.exp(scores), 0.0)
    weights = (expon / jnp.sum(expon, axis=-1, keepdims=True)).astype(jnp.bfloat16)
    attended = jnp.einsum("phqk,pkhd->pqhd", weights, values_enc, preferred_element_type=jnp.float32)
    attended = attended.astype(jnp.bfloat16).reshape(tok_rows, local_cols)
    attended = jnp.concatenate(in_order(attended, swap(attended, "xl"), "xl"), axis=1)
    partial_value = mm(attended, wo_full).astype(jnp.bfloat16)
    summed = partial_value.astype(jnp.float32) + swap(partial_value, "c").astype(jnp.float32)
    encoded = (floats + summed).astype(jnp.bfloat16)
    final = rms_norm(encoded.astype(jnp.float32), final_gain).astype(jnp.bfloat16)
    dkeys = by_heads(mm(final, dwk))
    dvalues_wide = by_heads(mm(final, dwv)).astype(jnp.float32)
    question_count, dec_len, _ = dec_query.shape
    member = owner[:, None] == lax.broadcasted_iota(jnp.int32, (pass_count, question_count), 1)
    member_float = member.astype(jnp.float32)
    picked = dec_query[owner].reshape(pass_count, dec_len, local_heads, HD)
    dec_scores = jnp.einsum("pthd,plhd->pthl", picked, dkeys, preferred_element_type=jnp.float32) * SCALE
    dec_expon = jnp.where(visible[:, None, None, :], jnp.exp(dec_scores), 0.0)
    passage_total = jnp.sum(dec_expon, axis=-1)
    passage_numer = jnp.einsum("pthl,plhd->pthd", dec_expon, dvalues_wide, precision=lax.Precision.HIGHEST)
    question_numer = jnp.einsum("pq,pthd->qthd", member_float, passage_numer, precision=lax.Precision.HIGHEST)
    question_total = jnp.einsum("pq,pth->qth", member_float, passage_total, precision=lax.Precision.HIGHEST)
    numer_out = question_numer.reshape(question_count, dec_len, local_cols).astype(jnp.bfloat16)
    total_out = question_total.reshape(question_count, 1, dec_len * local_heads).astype(jnp.bfloat16)
    total_out = jnp.pad(total_out, ((0, 0), (0, 0), (0, local_cols - dec_len * local_heads)))
    sent = jnp.concatenate([numer_out, total_out], axis=1)
    came = lax.all_to_all(sent, DP, 0, 0, tiled=True).astype(jnp.float32)
    came = jnp.sum(came, axis=0)
    own_numer = came[:dec_len].reshape(dec_len, local_heads, HD)
    own_total = came[dec_len, : dec_len * local_heads].reshape(dec_len, local_heads, 1)
    context = (own_numer / own_total).astype(jnp.bfloat16).reshape(1, dec_len, local_cols)
    return (encoded.reshape(pass_count, seq_len, width), context)


def solution(mesh):
    fine = Mesh(mesh.devices.reshape(SIZES), AXES)
    row = P(DP, MP)
    return jax.shard_map(
        shards,
        mesh=fine,
        in_specs=(
            P(DP, None, None),
            P(DP),
            P(DP),
            P(),
            P(),
            row,
            row,
            row,
            P(MP, DP),
            row,
            row,
            P(None, None, MP),
        ),
        out_specs=(P(DP, None, None), P(DP, None, MP)),
        check_vma=False,
    )
```

```python
import functools

import jax
import jax.numpy as jnp
from jax import lax
from jax.experimental import pallas as pl
from jax.experimental.pallas import tpu as pltpu
from jax.sharding import Mesh, PartitionSpec as P

HD = 64
EPS = 1e-06
SCALE = 0.125
AXES = ("y", "xh", "z", "xl", "c")
NY, NXH, NZ, NXL, NC = 4, 2, 4, 2, 2
DP = ("y", "xh", "z")
MP = ("xl", "c")
SEQ = 128
PAIR = 2 * HD
HALVES = 2
VMEM = 52 * 1024 * 1024


def swap(values, axis):
    return lax.ppermute(values, axis, [(0, 1), (1, 0)])


def in_order(mine, other, axis):
    first = lax.axis_index(axis) == 0
    return jnp.where(first, mine, other), jnp.where(first, other, mine)


def anywhere():
    return pl.BlockSpec(memory_space=pl.ANY)


def in_smem():
    return pl.BlockSpec(memory_space=pltpu.SMEM)


def dp_blocks():
    for y in range(NY):
        for xh in range(NXH):
            for z in range(NZ):
                yield y, xh, z, (y * NXH + xh) * NZ + z


def project(rows_ref, weight_ref, out_ref, count, cols):
    wide = 256

    def step(i, _):
        which = i // (cols // wide)
        at = pl.multiple_of((i % (cols // wide)) * wide, wide)
        acc = jnp.dot(rows_ref[...], weight_ref[which, :, pl.ds(at, wide)], preferred_element_type=jnp.float32)
        out_ref[which, :, pl.ds(at, wide)] = acc.astype(out_ref.dtype)
        return 0

    lax.fori_loop(0, count * (cols // wide), step, 0)


def attend_kernel(half, tokens, lens_ref, normed_ref, weights_ref, out_ref, rows, weight, qkv, sem_a, sem_w):
    count, width, cols = weight.shape
    copy_rows = pltpu.make_async_copy(normed_ref.at[pl.ds(half * tokens, tokens)], rows, sem_a)
    copy_rows.start()
    for which in range(count):
        for y, xh, z, d in dp_blocks():
            pltpu.make_async_copy(
                weights_ref.at[y * NZ + z, xh, which], weight.at[which, pl.ds(d * SEQ, SEQ)], sem_w.at[which]
            ).start()
    copy_rows.wait()
    wide = 256
    for which in range(count):
        pltpu.make_async_copy(weight.at[which], weight.at[which], sem_w.at[which]).wait()

        def step(i, _, which=which):
            at = pl.multiple_of(i * wide, wide)
            acc = jnp.dot(rows[...], weight[which, :, pl.ds(at, wide)], preferred_element_type=jnp.float32)
            qkv[which, :, pl.ds(at, wide)] = acc.astype(jnp.bfloat16)
            return 0

        lax.fori_loop(0, cols // wide, step, 0)

    lane = lax.broadcasted_iota(jnp.int32, (1, PAIR), 1)
    low = (lane < HD).astype(jnp.bfloat16)
    high = (lane >= HD).astype(jnp.bfloat16)

    def one(p, _):
        at = pl.multiple_of(p * SEQ, SEQ)
        seen = lane < lens_ref[half * (tokens // SEQ) + p]
        for hp in range(cols // PAIR):
            here = slice(hp * PAIR, (hp + 1) * PAIR)
            q = qkv[0, pl.ds(at, SEQ), here]
            k = qkv[1, pl.ds(at, SEQ), here]
            v = qkv[2, pl.ds(at, SEQ), here]
            q_two = jnp.concatenate([q * low, q * high], axis=0)
            scores = lax.dot_general(q_two, k, (((1,), (1,)), ((), ())), preferred_element_type=jnp.float32) * SCALE
            expon = jnp.where(seen, jnp.exp(scores), 0.0)
            share = (expon / jnp.sum(expon, axis=-1, keepdims=True)).astype(jnp.bfloat16)
            both = jnp.dot(share, v, preferred_element_type=jnp.float32)
            out_ref[pl.ds(at, SEQ), here] = jnp.where(lane < HD, both[:SEQ], both[SEQ:]).astype(jnp.bfloat16)
        return 0

    lax.fori_loop(0, tokens // SEQ, one, 0)


def attend(half, lengths, normed, gathered):
    total, width = normed.shape
    tokens = total // HALVES
    cols = gathered.shape[-1]
    return pl.pallas_call(
        functools.partial(attend_kernel, half, tokens),
        out_shape=jax.ShapeDtypeStruct((tokens, cols), jnp.bfloat16),
        in_specs=[in_smem(), anywhere(), anywhere()],
        out_specs=pl.BlockSpec(memory_space=pltpu.VMEM),
        scratch_shapes=[
            pltpu.VMEM((tokens, width), jnp.bfloat16),
            pltpu.VMEM((3, width, cols), jnp.bfloat16),
            pltpu.VMEM((3, tokens, cols), jnp.bfloat16),
            pltpu.SemaphoreType.DMA,
            pltpu.SemaphoreType.DMA((3,)),
        ],
        compiler_params=pltpu.CompilerParams(vmem_limit_bytes=VMEM),
        cost_estimate=pl.CostEstimate(flops=2 * tokens * width * cols * 3, bytes_accessed=18 << 20, transcendentals=tokens * SEQ * 8),
    )(lengths, normed, gathered)


def output_kernel(where_ref, mine_ref, other_ref, weights_ref, out_ref, rows, weight, sem_a, sem_w):
    tokens, cols = mine_ref.shape
    xl = where_ref[0]
    mine_at = pl.multiple_of(xl * cols, cols)
    other_at = pl.multiple_of((1 - xl) * cols, cols)
    pltpu.make_async_copy(mine_ref, rows.at[:, pl.ds(mine_at, cols)], sem_a).start()
    pltpu.make_async_copy(other_ref, rows.at[:, pl.ds(other_at, cols)], sem_a).start()
    for y, xh, z, d in dp_blocks():
        pltpu.make_async_copy(
            weights_ref.at[y * NZ + z, xh], weight.at[:, pl.ds(d * SEQ, SEQ)], sem_w.at[y]
        ).start()
    pltpu.make_async_copy(rows, rows, sem_a).wait()
    part = weight.shape[1] // NY
    wide = 256
    for y in range(NY):
        quarter = weight.at[:, pl.ds(y * part, part)]
        pltpu.make_async_copy(quarter, quarter, sem_w.at[y]).wait()

        def step(i, _, y=y):
            at = pl.multiple_of(y * part + i * wide, wide)
            acc = jnp.dot(rows[...], weight[:, pl.ds(at, wide)], preferred_element_type=jnp.float32)
            out_ref[:, pl.ds(at, wide)] = acc.astype(jnp.bfloat16)
            return 0

        lax.fori_loop(0, part // wide, step, 0)


def output(where, mine, other, gathered, width):
    tokens, cols = mine.shape
    return pl.pallas_call(
        output_kernel,
        out_shape=jax.ShapeDtypeStruct((tokens, width), jnp.bfloat16),
        in_specs=[in_smem(), anywhere(), anywhere(), anywhere()],
        out_specs=pl.BlockSpec(memory_space=pltpu.VMEM),
        scratch_shapes=[
            pltpu.VMEM((tokens, 2 * cols), jnp.bfloat16),
            pltpu.VMEM((2 * cols, width), jnp.bfloat16),
            pltpu.SemaphoreType.DMA,
            pltpu.SemaphoreType.DMA((NY,)),
        ],
        compiler_params=pltpu.CompilerParams(vmem_limit_bytes=VMEM),
        cost_estimate=pl.CostEstimate(flops=4 * tokens * width * cols, bytes_accessed=13 << 20, transcendentals=0),
    )(where, mine, other, gathered)


def decode_kernel(
    half, has_prior, lens_ref, owner_ref, gain_ref, query_ref, passages_ref, mine_ref, other_ref, weights_ref, *rest
):
    if has_prior:
        rest = rest[1:]
    encoded_ref, numer_ref, final, weight, kv, sem_w = rest
    step = pl.program_id(0)
    steps = final.shape[0] // SEQ
    count, width, cols = weight.shape

    @pl.when(step == 0)
    def _():
        for which in range(count):
            for y, xh, z, d in dp_blocks():
                pltpu.make_async_copy(
                    weights_ref.at[y * NZ + z, xh, which], weight.at[which, pl.ds(d * SEQ, SEQ)], sem_w.at[which]
                ).start()

    floats = passages_ref[...].astype(jnp.float32)
    summed = mine_ref[...].astype(jnp.float32) + other_ref[...].astype(jnp.float32)
    encoded = (floats + summed).astype(jnp.bfloat16)
    encoded_ref[...] = encoded
    values = encoded.astype(jnp.float32)
    mean = jnp.mean(values * values, axis=-1, keepdims=True)
    final[pl.ds(pl.multiple_of(step * SEQ, SEQ), SEQ), :] = (
        values * lax.rsqrt(mean + EPS) * gain_ref[...]
    ).astype(jnp.bfloat16)

    @pl.when(step == steps - 1)
    def _():
        wide = 256
        for which in range(count):
            pltpu.make_async_copy(weight.at[which], weight.at[which], sem_w.at[which]).wait()

            def column(i, _, which=which):
                at = pl.multiple_of(i * wide, wide)
                acc = jnp.dot(final[...], weight[which, :, pl.ds(at, wide)], preferred_element_type=jnp.float32)
                kv[which, :, pl.ds(at, wide)] = acc.astype(jnp.bfloat16)
                return 0

            lax.fori_loop(0, cols // wide, column, 0)

        lane = lax.broadcasted_iota(jnp.int32, (1, PAIR), 1)
        low = (lane < HD).astype(jnp.bfloat16)
        high = (lane >= HD).astype(jnp.bfloat16)
        dec_len = query_ref.shape[1]

        def one(p, _):
            at = pl.multiple_of(p * SEQ, SEQ)
            seen = lane < lens_ref[half * steps + p]
            question = owner_ref[half * steps + p]
            totals = jnp.zeros((dec_len, PAIR), jnp.float32)
            for hp in range(cols // PAIR):
                here = slice(hp * PAIR, (hp + 1) * PAIR)
                q = query_ref[question, :, here]
                k = kv[0, pl.ds(at, SEQ), here]
                v = kv[1, pl.ds(at, SEQ), here]
                q_two = jnp.concatenate([q * low, q * high], axis=0)
                scores = lax.dot_general(q_two, k, (((1,), (1,)), ((), ())), preferred_element_type=jnp.float32) * SCALE
                expon = jnp.where(seen, jnp.exp(scores), 0.0)
                total = jnp.sum(expon, axis=-1, keepdims=True)
                coarse = expon.astype(jnp.bfloat16)
                fine = (expon - coarse.astype(jnp.float32)).astype(jnp.bfloat16)
                both = jnp.dot(coarse, v, preferred_element_type=jnp.float32) + jnp.dot(
                    fine, v, preferred_element_type=jnp.float32
                )
                numer_ref[p, :, here] = jnp.where(lane < HD, both[:dec_len], both[dec_len:])
                totals = jnp.where(lane == 2 * hp, total[:dec_len], totals)
                totals = jnp.where(lane == 2 * hp + 1, total[dec_len:], totals)
            numer_ref[p, :, cols : cols + PAIR] = totals
            return 0

        lax.fori_loop(0, steps, one, 0)


def decode(half, lengths, owner, gain, query, passages, mine, other, gathered, prior):
    tokens, width = mine.shape
    cols = gathered.shape[-1]
    steps = tokens // SEQ
    questions, dec_len, _ = query.shape
    block = (SEQ, width)
    in_specs = [
        in_smem(),
        in_smem(),
        pl.BlockSpec((1, width), lambda i: (0, 0)),
        pl.BlockSpec((questions, dec_len, cols), lambda i: (0, 0, 0)),
        pl.BlockSpec(block, lambda i: (half * steps + i, 0)),
        pl.BlockSpec(block, lambda i: (i, 0)),
        pl.BlockSpec(block, lambda i: (i, 0)),
        anywhere(),
    ]
    args = [lengths, owner, gain, query, passages, mine, other, gathered]
    aliases = {}
    if prior is not None:
        in_specs.append(anywhere())
        args.append(prior)
        aliases = {8: 0}
    return pl.pallas_call(
        functools.partial(decode_kernel, half, prior is not None),
        grid=(steps,),
        out_shape=(
            jax.ShapeDtypeStruct(passages.shape, jnp.bfloat16),
            jax.ShapeDtypeStruct((steps, dec_len, cols + PAIR), jnp.float32),
        ),
        in_specs=in_specs,
        out_specs=(
            pl.BlockSpec(block, lambda i: (half * steps + i, 0)),
            pl.BlockSpec((steps, dec_len, cols + PAIR), lambda i: (0, 0, 0)),
        ),
        scratch_shapes=[
            pltpu.VMEM((tokens, width), jnp.bfloat16),
            pltpu.VMEM((2, width, cols), jnp.bfloat16),
            pltpu.VMEM((2, tokens, cols), jnp.bfloat16),
            pltpu.SemaphoreType.DMA((2,)),
        ],
        input_output_aliases=aliases,
        compiler_params=pltpu.CompilerParams(vmem_limit_bytes=VMEM),
        cost_estimate=pl.CostEstimate(flops=4 * tokens * width * cols, bytes_accessed=24 << 20, transcendentals=1 << 17),
    )(*args)


def place_kernel(owner_ref, *refs):
    parts, out_ref, acc = refs[:HALVES], refs[HALVES], refs[HALVES + 1]
    acc[...] = jnp.zeros_like(acc)
    count = parts[0].shape[0]
    for half in range(HALVES):
        for p in range(count):
            question = owner_ref[half * count + p]
            acc[question] = acc[question] + parts[half][p]
    out_ref[...] = acc[...].astype(jnp.bfloat16)


def place(owner, parts, questions):
    shape = (questions,) + parts[0].shape[1:]
    return pl.pallas_call(
        place_kernel,
        out_shape=jax.ShapeDtypeStruct(shape, jnp.bfloat16),
        in_specs=[in_smem()] + [pl.BlockSpec(memory_space=pltpu.VMEM)] * HALVES,
        out_specs=pl.BlockSpec(memory_space=pltpu.VMEM),
        scratch_shapes=[pltpu.VMEM(shape, jnp.float32)],
        compiler_params=pltpu.CompilerParams(vmem_limit_bytes=VMEM),
        cost_estimate=pl.CostEstimate(flops=1 << 20, bytes_accessed=2 << 20, transcendentals=0),
    )(owner, *parts)


def gather_rows(parts):
    both = jnp.stack(in_order(parts, swap(parts, "xh"), "xh"))
    return lax.all_gather(both, ("y", "z"), axis=0, tiled=False).reshape((NY * NZ,) + both.shape)


def shards(
    passages,
    lengths,
    owner,
    enc_gain,
    final_gain,
    enc_wq,
    enc_wk,
    enc_wv,
    enc_wo,
    dec_wk,
    dec_wv,
    dec_query,
):
    pass_count, seq_len, width = passages.shape
    tok_rows = pass_count * seq_len
    local_cols = enc_wq.shape[1]
    local_heads = local_cols // HD
    question_count, dec_len, _ = dec_query.shape
    flat = passages.reshape(tok_rows, width)
    floats = flat.astype(jnp.float32)
    mean = jnp.mean(floats * floats, axis=-1, keepdims=True)
    normed = (floats * lax.rsqrt(mean + EPS) * enc_gain).astype(jnp.bfloat16)

    qkv = gather_rows(jnp.stack([enc_wq, enc_wk, enc_wv]))
    wo_both = jnp.concatenate(in_order(enc_wo, swap(enc_wo, "xl"), "xl"), axis=0)
    wo = gather_rows(wo_both)
    dkv = gather_rows(jnp.stack([dec_wk, dec_wv]))

    where = lax.axis_index("xl").astype(jnp.int32).reshape(1)
    mine = [attend(half, lengths, normed, qkv) for half in range(HALVES)]
    theirs = [swap(part, "xl") for part in mine]
    partial = [output(where, mine[half], theirs[half], wo, width) for half in range(HALVES)]
    partial_other = [swap(part, "c") for part in partial]
    encoded = None
    numers = []
    for half in range(HALVES):
        encoded, numer = decode(
            half, lengths, owner, final_gain.reshape(1, width), dec_query, flat, partial[half], partial_other[half], dkv, encoded
        )
        numers.append(numer)
    sent = place(owner, numers, question_count)
    came = lax.all_to_all(sent, DP, 0, 0, tiled=True).astype(jnp.float32)
    came = jnp.sum(came, axis=0)
    own_numer = came[:, :local_cols].reshape(dec_len, local_heads, HD)
    own_total = came[:, local_cols : local_cols + local_heads].reshape(dec_len, local_heads, 1)
    context = (own_numer / own_total).astype(jnp.bfloat16).reshape(1, dec_len, local_cols)
    return (encoded.reshape(pass_count, seq_len, width), context)


def solution(mesh):
    fine = Mesh(mesh.devices.reshape((NY, NXH, NZ, NXL, NC)), AXES)
    row = P(DP, MP)
    return jax.shard_map(
        shards,
        mesh=fine,
        in_specs=(
            P(DP, None, None),
            P(DP),
            P(DP),
            P(),
            P(),
            row,
            row,
            row,
            P(MP, DP),
            row,
            row,
            P(None, None, MP),
        ),
        out_specs=(P(DP, None, None), P(DP, None, MP)),
        check_vma=False,
    )
```

```python
import functools

import jax
import jax.numpy as jnp
from jax import lax
from jax.experimental import pallas as pl
from jax.experimental.pallas import tpu as pltpu
from jax.sharding import Mesh, PartitionSpec as P

HD = 64
EPS = 1e-06
SCALE = 0.125
AXES = ("y", "xh", "z", "xl", "c")
NY, NXH, NZ, NXL, NC = 4, 2, 4, 2, 2
DP = ("y", "xh", "z")
MP = ("xl", "c")
SEQ = 128
PAIR = 2 * HD
HALVES = 2
VMEM = 52 * 1024 * 1024


def swap(values, axis):
    return lax.ppermute(values, axis, [(0, 1), (1, 0)])


def in_order(mine, other, axis):
    first = lax.axis_index(axis) == 0
    return jnp.where(first, mine, other), jnp.where(first, other, mine)


RING = (0, 3, 1, 2)
X_OFFSETS = ((0, 0), (3, 0), (1, 0), (2, 0), (2, 2))


def shift(values, axis, by):
    size = lax.axis_size(axis)
    return lax.ppermute(values, axis, [(i, (i + by) % size) for i in range(size)])


def ring_gather(values, axis):
    return jnp.stack([values, shift(values, axis, 1), shift(values, axis, -1), shift(values, axis, 2)])


def x_ring_pieces(values):
    below, above = shift(values, ("xh", "xl"), 1), shift(values, ("xh", "xl"), -1)
    half = values.shape[0] // 2
    return [
        values,
        below,
        above,
        shift(below[:half], ("xh", "xl"), 1),
        shift(above[half:], ("xh", "xl"), -1),
    ]


def anywhere():
    return pl.BlockSpec(memory_space=pl.ANY)


def in_smem():
    return pl.BlockSpec(memory_space=pltpu.SMEM)


def dp_blocks():
    for y in range(NY):
        for xh in range(NXH):
            for z in range(NZ):
                yield y, xh, z, (y * NXH + xh) * NZ + z


def project(rows_ref, weight_ref, out_ref, count, cols):
    wide = 256

    def step(i, _):
        which = i // (cols // wide)
        at = pl.multiple_of((i % (cols // wide)) * wide, wide)
        acc = jnp.dot(rows_ref[...], weight_ref[which, :, pl.ds(at, wide)], preferred_element_type=jnp.float32)
        out_ref[which, :, pl.ds(at, wide)] = acc.astype(out_ref.dtype)
        return 0

    lax.fori_loop(0, count * (cols // wide), step, 0)


def attend_kernel(half, tokens, lens_ref, normed_ref, weights_ref, out_ref, rows, weight, qkv, sem_a, sem_w):
    count, width, cols = weight.shape
    copy_rows = pltpu.make_async_copy(normed_ref.at[pl.ds(half * tokens, tokens)], rows, sem_a)
    copy_rows.start()
    for which in range(count):
        for y, xh, z, d in dp_blocks():
            pltpu.make_async_copy(
                weights_ref.at[y * NZ + z, xh, which], weight.at[which, pl.ds(d * SEQ, SEQ)], sem_w.at[which]
            ).start()
    copy_rows.wait()
    wide = 256
    for which in range(count):
        pltpu.make_async_copy(weight.at[which], weight.at[which], sem_w.at[which]).wait()

        def step(i, _, which=which):
            at = pl.multiple_of(i * wide, wide)
            acc = jnp.dot(rows[...], weight[which, :, pl.ds(at, wide)], preferred_element_type=jnp.float32)
            qkv[which, :, pl.ds(at, wide)] = acc.astype(jnp.bfloat16)
            return 0

        lax.fori_loop(0, cols // wide, step, 0)

    lane = lax.broadcasted_iota(jnp.int32, (1, PAIR), 1)
    low = (lane < HD).astype(jnp.bfloat16)
    high = (lane >= HD).astype(jnp.bfloat16)

    def one(p, _):
        at = pl.multiple_of(p * SEQ, SEQ)
        seen = lane < lens_ref[half * (tokens // SEQ) + p]
        for hp in range(cols // PAIR):
            here = slice(hp * PAIR, (hp + 1) * PAIR)
            q = qkv[0, pl.ds(at, SEQ), here]
            k = qkv[1, pl.ds(at, SEQ), here]
            v = qkv[2, pl.ds(at, SEQ), here]
            q_two = jnp.concatenate([q * low, q * high], axis=0)
            scores = lax.dot_general(q_two, k, (((1,), (1,)), ((), ())), preferred_element_type=jnp.float32) * SCALE
            expon = jnp.where(seen, jnp.exp(scores), 0.0)
            share = (expon / jnp.sum(expon, axis=-1, keepdims=True)).astype(jnp.bfloat16)
            both = jnp.dot(share, v, preferred_element_type=jnp.float32)
            out_ref[pl.ds(at, SEQ), here] = jnp.where(lane < HD, both[:SEQ], both[SEQ:]).astype(jnp.bfloat16)
        return 0

    lax.fori_loop(0, tokens // SEQ, one, 0)


def attend(half, lengths, normed, gathered):
    total, width = normed.shape
    tokens = total // HALVES
    cols = gathered.shape[-1]
    return pl.pallas_call(
        functools.partial(attend_kernel, half, tokens),
        out_shape=jax.ShapeDtypeStruct((tokens, cols), jnp.bfloat16),
        in_specs=[in_smem(), anywhere(), anywhere()],
        out_specs=pl.BlockSpec(memory_space=pltpu.VMEM),
        scratch_shapes=[
            pltpu.VMEM((tokens, width), jnp.bfloat16),
            pltpu.VMEM((3, width, cols), jnp.bfloat16),
            pltpu.VMEM((3, tokens, cols), jnp.bfloat16),
            pltpu.SemaphoreType.DMA,
            pltpu.SemaphoreType.DMA((3,)),
        ],
        compiler_params=pltpu.CompilerParams(vmem_limit_bytes=VMEM),
        cost_estimate=pl.CostEstimate(flops=2 * tokens * width * cols * 3, bytes_accessed=18 << 20, transcendentals=tokens * SEQ * 8),
    )(lengths, normed, gathered)


def output_kernel(where_ref, mine_ref, other_ref, *rest):
    pieces, (out_ref, rows, weight, sem_a, sem_w) = rest[: len(X_OFFSETS)], rest[len(X_OFFSETS) :]
    tokens, cols = mine_ref.shape
    y, xh, z, xl = (where_ref[i] for i in range(4))
    mine_at = pl.multiple_of(xl * cols, cols)
    other_at = pl.multiple_of((1 - xl) * cols, cols)
    pltpu.make_async_copy(mine_ref, rows.at[:, pl.ds(mine_at, cols)], sem_a).start()
    pltpu.make_async_copy(other_ref, rows.at[:, pl.ds(other_at, cols)], sem_a).start()
    for piece, (dx, first) in zip(pieces, X_OFFSETS):
        x_from = lax.rem(xh * NXL + xl + dx, NXH * NXL)
        row = pl.multiple_of(lax.rem(x_from, NXL) * cols, cols)
        for i in range(piece.shape[0]):
            z_from = lax.rem(z + RING[first + i], NZ)
            for j in range(NY):
                y_from = lax.rem(y + RING[j], NY)
                block = (y_from * NXH + x_from // NXL) * NZ + z_from
                at = pl.multiple_of(block * SEQ, SEQ)
                pltpu.make_async_copy(
                    piece.at[i, j], weight.at[pl.ds(row, cols), pl.ds(at, SEQ)], sem_w.at[y_from]
                ).start()
    pltpu.make_async_copy(rows, rows, sem_a).wait()
    part = weight.shape[1] // NY
    wide = 256
    for q in range(NY):
        quarter = weight.at[:, pl.ds(q * part, part)]
        pltpu.make_async_copy(quarter, quarter, sem_w.at[q]).wait()

        def step(i, _, q=q):
            at = pl.multiple_of(q * part + i * wide, wide)
            acc = jnp.dot(rows[...], weight[:, pl.ds(at, wide)], preferred_element_type=jnp.float32)
            out_ref[:, pl.ds(at, wide)] = acc.astype(jnp.bfloat16)
            return 0

        lax.fori_loop(0, part // wide, step, 0)


def output(where, mine, other, pieces, width):
    tokens, cols = mine.shape
    return pl.pallas_call(
        output_kernel,
        out_shape=jax.ShapeDtypeStruct((tokens, width), jnp.bfloat16),
        in_specs=[in_smem()] + [anywhere()] * (2 + len(pieces)),
        out_specs=pl.BlockSpec(memory_space=pltpu.VMEM),
        scratch_shapes=[
            pltpu.VMEM((tokens, 2 * cols), jnp.bfloat16),
            pltpu.VMEM((2 * cols, width), jnp.bfloat16),
            pltpu.SemaphoreType.DMA,
            pltpu.SemaphoreType.DMA((NY,)),
        ],
        compiler_params=pltpu.CompilerParams(vmem_limit_bytes=VMEM),
        cost_estimate=pl.CostEstimate(flops=4 * tokens * width * cols, bytes_accessed=13 << 20, transcendentals=0),
    )(where, mine, other, *pieces)


def decode_kernel(
    half, has_prior, lens_ref, owner_ref, gain_ref, query_ref, passages_ref, mine_ref, other_ref, weights_ref, *rest
):
    if has_prior:
        rest = rest[1:]
    encoded_ref, numer_ref, final, weight, kv, sem_w = rest
    step = pl.program_id(0)
    steps = final.shape[0] // SEQ
    count, width, cols = weight.shape

    @pl.when(step == 0)
    def _():
        for which in range(count):
            for y, xh, z, d in dp_blocks():
                pltpu.make_async_copy(
                    weights_ref.at[y * NZ + z, xh, which], weight.at[which, pl.ds(d * SEQ, SEQ)], sem_w.at[which]
                ).start()

    floats = passages_ref[...].astype(jnp.float32)
    summed = mine_ref[...].astype(jnp.float32) + other_ref[...].astype(jnp.float32)
    encoded = (floats + summed).astype(jnp.bfloat16)
    encoded_ref[...] = encoded
    values = encoded.astype(jnp.float32)
    mean = jnp.mean(values * values, axis=-1, keepdims=True)
    final[pl.ds(pl.multiple_of(step * SEQ, SEQ), SEQ), :] = (
        values * lax.rsqrt(mean + EPS) * gain_ref[...]
    ).astype(jnp.bfloat16)

    @pl.when(step == steps - 1)
    def _():
        wide = 256
        for which in range(count):
            pltpu.make_async_copy(weight.at[which], weight.at[which], sem_w.at[which]).wait()

            def column(i, _, which=which):
                at = pl.multiple_of(i * wide, wide)
                acc = jnp.dot(final[...], weight[which, :, pl.ds(at, wide)], preferred_element_type=jnp.float32)
                kv[which, :, pl.ds(at, wide)] = acc.astype(jnp.bfloat16)
                return 0

            lax.fori_loop(0, cols // wide, column, 0)

        lane = lax.broadcasted_iota(jnp.int32, (1, PAIR), 1)
        low = (lane < HD).astype(jnp.bfloat16)
        high = (lane >= HD).astype(jnp.bfloat16)
        dec_len = query_ref.shape[1]

        def one(p, _):
            at = pl.multiple_of(p * SEQ, SEQ)
            seen = lane < lens_ref[half * steps + p]
            question = owner_ref[half * steps + p]
            totals = jnp.zeros((dec_len, PAIR), jnp.float32)
            for hp in range(cols // PAIR):
                here = slice(hp * PAIR, (hp + 1) * PAIR)
                q = query_ref[question, :, here]
                k = kv[0, pl.ds(at, SEQ), here]
                v = kv[1, pl.ds(at, SEQ), here]
                q_two = jnp.concatenate([q * low, q * high], axis=0)
                scores = lax.dot_general(q_two, k, (((1,), (1,)), ((), ())), preferred_element_type=jnp.float32) * SCALE
                expon = jnp.where(seen, jnp.exp(scores), 0.0)
                total = jnp.sum(expon, axis=-1, keepdims=True)
                coarse = expon.astype(jnp.bfloat16)
                fine = (expon - coarse.astype(jnp.float32)).astype(jnp.bfloat16)
                both = jnp.dot(coarse, v, preferred_element_type=jnp.float32) + jnp.dot(
                    fine, v, preferred_element_type=jnp.float32
                )
                numer_ref[p, :, here] = jnp.where(lane < HD, both[:dec_len], both[dec_len:])
                totals = jnp.where(lane == 2 * hp, total[:dec_len], totals)
                totals = jnp.where(lane == 2 * hp + 1, total[dec_len:], totals)
            numer_ref[p, :, cols : cols + PAIR] = totals
            return 0

        lax.fori_loop(0, steps, one, 0)


def decode(half, lengths, owner, gain, query, passages, mine, other, gathered, prior):
    tokens, width = mine.shape
    cols = gathered.shape[-1]
    steps = tokens // SEQ
    questions, dec_len, _ = query.shape
    block = (SEQ, width)
    in_specs = [
        in_smem(),
        in_smem(),
        pl.BlockSpec((1, width), lambda i: (0, 0)),
        pl.BlockSpec((questions, dec_len, cols), lambda i: (0, 0, 0)),
        pl.BlockSpec(block, lambda i: (half * steps + i, 0)),
        pl.BlockSpec(block, lambda i: (i, 0)),
        pl.BlockSpec(block, lambda i: (i, 0)),
        anywhere(),
    ]
    args = [lengths, owner, gain, query, passages, mine, other, gathered]
    aliases = {}
    if prior is not None:
        in_specs.append(anywhere())
        args.append(prior)
        aliases = {8: 0}
    return pl.pallas_call(
        functools.partial(decode_kernel, half, prior is not None),
        grid=(steps,),
        out_shape=(
            jax.ShapeDtypeStruct(passages.shape, jnp.bfloat16),
            jax.ShapeDtypeStruct((steps, dec_len, cols + PAIR), jnp.float32),
        ),
        in_specs=in_specs,
        out_specs=(
            pl.BlockSpec(block, lambda i: (half * steps + i, 0)),
            pl.BlockSpec((steps, dec_len, cols + PAIR), lambda i: (0, 0, 0)),
        ),
        scratch_shapes=[
            pltpu.VMEM((tokens, width), jnp.bfloat16),
            pltpu.VMEM((2, width, cols), jnp.bfloat16),
            pltpu.VMEM((2, tokens, cols), jnp.bfloat16),
            pltpu.SemaphoreType.DMA((2,)),
        ],
        input_output_aliases=aliases,
        compiler_params=pltpu.CompilerParams(vmem_limit_bytes=VMEM),
        cost_estimate=pl.CostEstimate(flops=4 * tokens * width * cols, bytes_accessed=24 << 20, transcendentals=1 << 17),
    )(*args)


def place_kernel(owner_ref, *refs):
    parts, out_ref, acc = refs[:HALVES], refs[HALVES], refs[HALVES + 1]
    acc[...] = jnp.zeros_like(acc)
    count = parts[0].shape[0]
    for half in range(HALVES):
        for p in range(count):
            question = owner_ref[half * count + p]
            acc[question] = acc[question] + parts[half][p]
    out_ref[...] = acc[...].astype(jnp.bfloat16)


def place(owner, parts, questions):
    shape = (questions,) + parts[0].shape[1:]
    return pl.pallas_call(
        place_kernel,
        out_shape=jax.ShapeDtypeStruct(shape, jnp.bfloat16),
        in_specs=[in_smem()] + [pl.BlockSpec(memory_space=pltpu.VMEM)] * HALVES,
        out_specs=pl.BlockSpec(memory_space=pltpu.VMEM),
        scratch_shapes=[pltpu.VMEM(shape, jnp.float32)],
        compiler_params=pltpu.CompilerParams(vmem_limit_bytes=VMEM),
        cost_estimate=pl.CostEstimate(flops=1 << 20, bytes_accessed=2 << 20, transcendentals=0),
    )(owner, *parts)


def gather_rows(parts):
    both = jnp.stack(in_order(parts, swap(parts, "xh"), "xh"))
    return lax.all_gather(both, ("y", "z"), axis=0, tiled=False).reshape((NY * NZ,) + both.shape)


def shards(
    passages,
    lengths,
    owner,
    enc_gain,
    final_gain,
    enc_wq,
    enc_wk,
    enc_wv,
    enc_wo,
    dec_wk,
    dec_wv,
    dec_query,
):
    pass_count, seq_len, width = passages.shape
    tok_rows = pass_count * seq_len
    local_cols = enc_wq.shape[1]
    local_heads = local_cols // HD
    question_count, dec_len, _ = dec_query.shape
    flat = passages.reshape(tok_rows, width)
    floats = flat.astype(jnp.float32)
    mean = jnp.mean(floats * floats, axis=-1, keepdims=True)
    normed = (floats * lax.rsqrt(mean + EPS) * enc_gain).astype(jnp.bfloat16)

    qkv = gather_rows(jnp.stack([enc_wq, enc_wk, enc_wv]))
    wo = x_ring_pieces(ring_gather(ring_gather(enc_wo, "y"), "z"))
    dkv = gather_rows(jnp.stack([dec_wk, dec_wv]))

    where = jnp.stack([lax.axis_index(axis) for axis in AXES]).astype(jnp.int32)
    mine = [attend(half, lengths, normed, qkv) for half in range(HALVES)]
    theirs = [swap(part, "xl") for part in mine]
    partial = [output(where, mine[half], theirs[half], wo, width) for half in range(HALVES)]
    partial_other = [swap(part, "c") for part in partial]
    encoded = None
    numers = []
    for half in range(HALVES):
        encoded, numer = decode(
            half, lengths, owner, final_gain.reshape(1, width), dec_query, flat, partial[half], partial_other[half], dkv, encoded
        )
        numers.append(numer)
    sent = place(owner, numers, question_count)
    came = lax.all_to_all(sent, DP, 0, 0, tiled=True).astype(jnp.float32)
    came = jnp.sum(came, axis=0)
    own_numer = came[:, :local_cols].reshape(dec_len, local_heads, HD)
    own_total = came[:, local_cols : local_cols + local_heads].reshape(dec_len, local_heads, 1)
    context = (own_numer / own_total).astype(jnp.bfloat16).reshape(1, dec_len, local_cols)
    return (encoded.reshape(pass_count, seq_len, width), context)


def solution(mesh):
    fine = Mesh(mesh.devices.reshape((NY, NXH, NZ, NXL, NC)), AXES)
    row = P(DP, MP)
    return jax.shard_map(
        shards,
        mesh=fine,
        in_specs=(
            P(DP, None, None),
            P(DP),
            P(DP),
            P(),
            P(),
            row,
            row,
            row,
            P(MP, DP),
            row,
            row,
            P(None, None, MP),
        ),
        out_specs=(P(DP, None, None), P(DP, None, MP)),
        check_vma=False,
    )
```

```python
import functools

import jax
import jax.numpy as jnp
from jax import lax
from jax.experimental import pallas as pl
from jax.experimental.pallas import tpu as pltpu
from jax.sharding import Mesh, PartitionSpec as P

HD = 64
EPS = 1e-06
SCALE = 0.125
AXES = ("y", "xh", "z", "xl", "c")
NY, NXH, NZ, NXL, NC = 4, 2, 4, 2, 2
DP = ("y", "xh", "z")
MP = ("xl", "c")
SEQ = 128
PAIR = 2 * HD
HALVES = 2
VMEM = 52 * 1024 * 1024


def swap(values, axis):
    return lax.ppermute(values, axis, [(0, 1), (1, 0)])


RING = (0, 3, 1, 2)
X_OFFSETS = ((0, 0), (3, 0), (1, 0), (2, 0), (2, 2))


def shift(values, axis, by):
    size = lax.axis_size(axis)
    return lax.ppermute(values, axis, [(i, (i + by) % size) for i in range(size)])


def ring_gather(values, axis):
    return jnp.stack([values, shift(values, axis, 1), shift(values, axis, -1), shift(values, axis, 2)])


def x_ring_pieces(values):
    below, above = shift(values, ("xh", "xl"), 1), shift(values, ("xh", "xl"), -1)
    half = values.shape[0] // 2
    return [
        values,
        below,
        above,
        shift(below[:half], ("xh", "xl"), 1),
        shift(above[half:], ("xh", "xl"), -1),
    ]


def anywhere():
    return pl.BlockSpec(memory_space=pl.ANY)


def in_smem():
    return pl.BlockSpec(memory_space=pltpu.SMEM)


def load_weights(where_ref, gathered_ref, weight, sem_w):
    xh = where_ref[1]
    for which in range(weight.shape[0]):
        for y in range(NY):
            for j in range(NXH):
                xh_from = xh if j == 0 else 1 - xh
                pltpu.make_async_copy(
                    gathered_ref.at[pl.ds(y * NZ, NZ), j, which],
                    weight.at[which, pl.ds((y * NXH + xh_from) * NZ, NZ)],
                    sem_w.at[which],
                ).start()


def attend_kernel(half, where_ref, lens_ref, normed_ref, weights_ref, out_ref, rows, weight, qkv, sem_a, sem_w):
    count, blocks, _, cols = weight.shape
    tokens = rows.shape[0]
    copy_rows = pltpu.make_async_copy(normed_ref.at[pl.ds(half * tokens, tokens)], rows, sem_a)
    copy_rows.start()
    load_weights(where_ref, weights_ref, weight, sem_w)
    copy_rows.wait()
    wide = 512
    for which in range(count):
        pltpu.make_async_copy(weight.at[which], weight.at[which], sem_w.at[which]).wait()

        def step(i, _, which=which):
            at = pl.multiple_of(i * wide, wide)
            acc = jnp.dot(
                rows[...],
                weight[which, :, :, pl.ds(at, wide)].reshape(blocks * SEQ, wide),
                preferred_element_type=jnp.float32,
            )
            qkv[which, :, pl.ds(at, wide)] = acc.astype(jnp.bfloat16)
            return 0

        lax.fori_loop(0, cols // wide, step, 0)

    lane = lax.broadcasted_iota(jnp.int32, (1, PAIR), 1)
    low = (lane < HD).astype(jnp.bfloat16)
    high = (lane >= HD).astype(jnp.bfloat16)

    def one(p, _):
        at = pl.multiple_of(p * SEQ, SEQ)
        seen = lane < lens_ref[half * (tokens // SEQ) + p]
        for hp in range(cols // PAIR):
            here = slice(hp * PAIR, (hp + 1) * PAIR)
            q = qkv[0, pl.ds(at, SEQ), here]
            k = qkv[1, pl.ds(at, SEQ), here]
            v = qkv[2, pl.ds(at, SEQ), here]
            q_two = jnp.concatenate([q * low, q * high], axis=0)
            scores = lax.dot_general(q_two, k, (((1,), (1,)), ((), ())), preferred_element_type=jnp.float32) * SCALE
            expon = jnp.where(seen, jnp.exp(scores), 0.0)
            share = (expon / jnp.sum(expon, axis=-1, keepdims=True)).astype(jnp.bfloat16)
            both = jnp.dot(share, v, preferred_element_type=jnp.float32)
            out_ref[pl.ds(at, SEQ), here] = jnp.where(lane < HD, both[:SEQ], both[SEQ:]).astype(jnp.bfloat16)
        return 0

    lax.fori_loop(0, tokens // SEQ, one, 0)


def attend(half, where, lengths, normed, gathered):
    total, width = normed.shape
    tokens = total // HALVES
    cols = gathered.shape[-1]
    return pl.pallas_call(
        functools.partial(attend_kernel, half),
        out_shape=jax.ShapeDtypeStruct((tokens, cols), jnp.bfloat16),
        in_specs=[in_smem(), in_smem(), anywhere(), anywhere()],
        out_specs=pl.BlockSpec(memory_space=pltpu.VMEM),
        scratch_shapes=[
            pltpu.VMEM((tokens, width), jnp.bfloat16),
            pltpu.VMEM((3, width // SEQ, SEQ, cols), jnp.bfloat16),
            pltpu.VMEM((3, tokens, cols), jnp.bfloat16),
            pltpu.SemaphoreType.DMA,
            pltpu.SemaphoreType.DMA((3,)),
        ],
        compiler_params=pltpu.CompilerParams(vmem_limit_bytes=VMEM),
        cost_estimate=pl.CostEstimate(flops=2 * tokens * width * cols * 3, bytes_accessed=18 << 20, transcendentals=tokens * SEQ * 8),
    )(where, lengths, normed, gathered)


def output_kernel(where_ref, mine_ref, other_ref, *rest):
    pieces, (out_ref, rows, weight, sem_a, sem_w) = rest[: len(X_OFFSETS)], rest[len(X_OFFSETS) :]
    tokens, cols = mine_ref.shape
    y, xh, z, xl = (where_ref[i] for i in range(4))
    mine_at = pl.multiple_of(xl * cols, cols)
    other_at = pl.multiple_of((1 - xl) * cols, cols)
    pltpu.make_async_copy(mine_ref, rows.at[:, pl.ds(mine_at, cols)], sem_a).start()
    pltpu.make_async_copy(other_ref, rows.at[:, pl.ds(other_at, cols)], sem_a).start()
    for piece, (dx, first) in zip(pieces, X_OFFSETS):
        x_from = lax.rem(xh * NXL + xl + dx, NXH * NXL)
        row = pl.multiple_of(lax.rem(x_from, NXL) * cols, cols)
        for i in range(piece.shape[0]):
            z_from = lax.rem(z + RING[first + i], NZ)
            for j in range(NY):
                y_from = lax.rem(y + RING[j], NY)
                block = (y_from * NXH + x_from // NXL) * NZ + z_from
                at = pl.multiple_of(block * SEQ, SEQ)
                pltpu.make_async_copy(
                    piece.at[i, j], weight.at[pl.ds(row, cols), pl.ds(at, SEQ)], sem_w.at[y_from]
                ).start()
    pltpu.make_async_copy(rows, rows, sem_a).wait()
    part = weight.shape[1] // NY
    wide = 512
    for q in range(NY):
        quarter = weight.at[:, pl.ds(q * part, part)]
        pltpu.make_async_copy(quarter, quarter, sem_w.at[q]).wait()

        def step(i, _, q=q):
            at = pl.multiple_of(q * part + i * wide, wide)
            acc = jnp.dot(rows[...], weight[:, pl.ds(at, wide)], preferred_element_type=jnp.float32)
            out_ref[:, pl.ds(at, wide)] = acc.astype(jnp.bfloat16)
            return 0

        lax.fori_loop(0, part // wide, step, 0)


def output(where, mine, other, pieces, width):
    tokens, cols = mine.shape
    return pl.pallas_call(
        output_kernel,
        out_shape=jax.ShapeDtypeStruct((tokens, width), jnp.bfloat16),
        in_specs=[in_smem()] + [anywhere()] * (2 + len(pieces)),
        out_specs=pl.BlockSpec(memory_space=pltpu.VMEM),
        scratch_shapes=[
            pltpu.VMEM((tokens, 2 * cols), jnp.bfloat16),
            pltpu.VMEM((2 * cols, width), jnp.bfloat16),
            pltpu.SemaphoreType.DMA,
            pltpu.SemaphoreType.DMA((NY,)),
        ],
        compiler_params=pltpu.CompilerParams(vmem_limit_bytes=VMEM),
        cost_estimate=pl.CostEstimate(flops=4 * tokens * width * cols, bytes_accessed=13 << 20, transcendentals=0),
    )(where, mine, other, *pieces)


def encode_kernel(gain_ref, passages_ref, mine_ref, other_ref, *rest):
    encoded_ref, final_ref = rest[-2:]
    floats = passages_ref[...].astype(jnp.float32)
    summed = mine_ref[...].astype(jnp.float32) + other_ref[...].astype(jnp.float32)
    encoded = (floats + summed).astype(jnp.bfloat16)
    encoded_ref[...] = encoded
    values = encoded.astype(jnp.float32)
    mean = jnp.mean(values * values, axis=-1, keepdims=True)
    final_ref[...] = (values * lax.rsqrt(mean + EPS) * gain_ref[...]).astype(jnp.bfloat16)


def encode(half, gain, passages, mine, other, prior):
    tokens, width = mine.shape
    steps = tokens // SEQ
    block = (SEQ, width)
    in_specs = [
        pl.BlockSpec((1, width), lambda i: (0, 0)),
        pl.BlockSpec(block, lambda i: (half * steps + i, 0)),
        pl.BlockSpec(block, lambda i: (i, 0)),
        pl.BlockSpec(block, lambda i: (i, 0)),
    ]
    args = [gain, passages, mine, other]
    aliases = {}
    if prior is not None:
        in_specs += [anywhere()]
        args += [prior]
        aliases = {4: 0}
    return pl.pallas_call(
        encode_kernel,
        grid=(steps,),
        out_shape=(
            jax.ShapeDtypeStruct(passages.shape, jnp.bfloat16),
            jax.ShapeDtypeStruct((tokens, width), jnp.bfloat16),
        ),
        in_specs=in_specs,
        out_specs=(pl.BlockSpec(block, lambda i: (half * steps + i, 0)), pl.BlockSpec(block, lambda i: (i, 0))),
        input_output_aliases=aliases,
        compiler_params=pltpu.CompilerParams(vmem_limit_bytes=32 * 1024 * 1024),
        cost_estimate=pl.CostEstimate(flops=8 * tokens * width, bytes_accessed=20 << 20, transcendentals=0),
    )(*args)


def decode_kernel(where_ref, lens_ref, owner_ref, query_ref, *rest):
    finals, rest = rest[:HALVES], rest[HALVES:]
    weights_ref, sent_ref, final, weight, kv, numer, sem_a, sem_w = rest
    count, blocks, _, cols = weight.shape
    tokens = final.shape[1]
    for half in range(HALVES):
        pltpu.make_async_copy(finals[half], final.at[half], sem_a.at[half]).start()
    load_weights(where_ref, weights_ref, weight, sem_w)
    numer[...] = jnp.zeros_like(numer)

    lane = lax.broadcasted_iota(jnp.int32, (1, PAIR), 1)
    low = (lane < HD).astype(jnp.bfloat16)
    high = (lane >= HD).astype(jnp.bfloat16)
    dec_len = query_ref.shape[1]
    wide = 256
    for half in range(HALVES):
        pltpu.make_async_copy(final.at[half], final.at[half], sem_a.at[half]).wait()
        for which in range(count):
            if half == 0:
                pltpu.make_async_copy(weight.at[which], weight.at[which], sem_w.at[which]).wait()

            def column(i, _, which=which, half=half):
                at = pl.multiple_of(i * wide, wide)
                acc = jnp.dot(
                    final[half],
                    weight[which, :, :, pl.ds(at, wide)].reshape(blocks * SEQ, wide),
                    preferred_element_type=jnp.float32,
                )
                kv[which, :, pl.ds(at, wide)] = acc.astype(jnp.bfloat16)
                return 0

            lax.fori_loop(0, cols // wide, column, 0)

        def one(p, _, half=half):
            at = pl.multiple_of(p * SEQ, SEQ)
            seen = lane < lens_ref[half * (tokens // SEQ) + p]
            question = owner_ref[half * (tokens // SEQ) + p]
            totals = jnp.zeros((dec_len, PAIR), jnp.float32)
            for hp in range(cols // PAIR):
                here = slice(hp * PAIR, (hp + 1) * PAIR)
                q = query_ref[question, :, here]
                k = kv[0, pl.ds(at, SEQ), here]
                v = kv[1, pl.ds(at, SEQ), here]
                q_two = jnp.concatenate([q * low, q * high], axis=0)
                scores = lax.dot_general(q_two, k, (((1,), (1,)), ((), ())), preferred_element_type=jnp.float32) * SCALE
                expon = jnp.where(seen, jnp.exp(scores), 0.0)
                total = jnp.sum(expon, axis=-1, keepdims=True)
                coarse = expon.astype(jnp.bfloat16)
                fine = (expon - coarse.astype(jnp.float32)).astype(jnp.bfloat16)
                both = jnp.dot(coarse, v, preferred_element_type=jnp.float32) + jnp.dot(
                    fine, v, preferred_element_type=jnp.float32
                )
                numer[question, :, here] += jnp.where(lane < HD, both[:dec_len], both[dec_len:])
                totals = jnp.where(lane == 2 * hp, total[:dec_len], totals)
                totals = jnp.where(lane == 2 * hp + 1, total[dec_len:], totals)
            numer[question, :, cols : cols + PAIR] += totals
            return 0

        lax.fori_loop(0, tokens // SEQ, one, 0)
    sent_ref[...] = numer[...].astype(jnp.bfloat16)


def decode(where, lengths, owner, query, finals, gathered):
    tokens, width = finals[0].shape
    questions, dec_len, cols = query.shape
    shape = (questions, dec_len, cols + PAIR)
    return pl.pallas_call(
        decode_kernel,
        out_shape=jax.ShapeDtypeStruct(shape, jnp.bfloat16),
        in_specs=[in_smem()] * 3 + [pl.BlockSpec(memory_space=pltpu.VMEM)] + [anywhere()] * (HALVES + 1),
        out_specs=pl.BlockSpec(memory_space=pltpu.VMEM),
        scratch_shapes=[
            pltpu.VMEM((HALVES, tokens, width), jnp.bfloat16),
            pltpu.VMEM((2, width // SEQ, SEQ, cols), jnp.bfloat16),
            pltpu.VMEM((2, tokens, cols), jnp.bfloat16),
            pltpu.VMEM(shape, jnp.float32),
            pltpu.SemaphoreType.DMA((HALVES,)),
            pltpu.SemaphoreType.DMA((2,)),
        ],
        compiler_params=pltpu.CompilerParams(vmem_limit_bytes=VMEM),
        cost_estimate=pl.CostEstimate(
            flops=4 * HALVES * tokens * width * cols, bytes_accessed=18 << 20, transcendentals=1 << 18
        ),
    )(where, lengths, owner, query, *finals, gathered)


def gather_rows(mine, other):
    both = jnp.stack([mine, other])
    return lax.all_gather(both, ("y", "z"), axis=0, tiled=False).reshape((NY * NZ,) + both.shape)


def shards(
    passages,
    lengths,
    owner,
    enc_gain,
    final_gain,
    enc_wq,
    enc_wk,
    enc_wv,
    enc_wo,
    dec_wk,
    dec_wv,
    dec_query,
):
    pass_count, seq_len, width = passages.shape
    tok_rows = pass_count * seq_len
    local_cols = enc_wq.shape[1]
    local_heads = local_cols // HD
    dec_len = dec_query.shape[1]
    flat = passages.reshape(tok_rows, width)
    floats = flat.astype(jnp.float32)
    mean = jnp.mean(floats * floats, axis=-1, keepdims=True)
    normed = (floats * lax.rsqrt(mean + EPS) * enc_gain).astype(jnp.bfloat16)

    enc = jnp.stack([enc_wq, enc_wk, enc_wv])
    enc_other = swap(enc, "xh")
    wo = ring_gather(enc_wo, "y")
    enc, enc_other, wo = lax.optimization_barrier((enc, enc_other, wo))
    qkv = gather_rows(enc, enc_other)
    wo = ring_gather(wo, "z")
    dec, wo = lax.optimization_barrier((jnp.stack([dec_wk, dec_wv]), wo))
    dkv = gather_rows(dec, swap(dec, "xh"))
    wo = x_ring_pieces(wo)
    where = jnp.stack([lax.axis_index(axis) for axis in AXES]).astype(jnp.int32)
    mine = [attend(half, where, lengths, normed, qkv) for half in range(HALVES)]
    theirs = [swap(part, "xl") for part in mine]
    partial = [output(where, mine[half], theirs[half], wo, width) for half in range(HALVES)]
    partial_other = [swap(part, "c") for part in partial]
    encoded = None
    finals = []
    for half in range(HALVES):
        encoded, final = encode(half, final_gain.reshape(1, width), flat, partial[half], partial_other[half], encoded)
        finals.append(final)
    sent = decode(where, lengths, owner, dec_query, finals, dkv)
    came = lax.all_to_all(sent, DP, 0, 0, tiled=True).astype(jnp.float32)
    came = jnp.sum(came, axis=0)
    own_numer = came[:, :local_cols].reshape(dec_len, local_heads, HD)
    own_total = came[:, local_cols : local_cols + local_heads].reshape(dec_len, local_heads, 1)
    context = (own_numer / own_total).astype(jnp.bfloat16).reshape(1, dec_len, local_cols)
    return (encoded.reshape(pass_count, seq_len, width), context)


def solution(mesh):
    fine = Mesh(mesh.devices.reshape((NY, NXH, NZ, NXL, NC)), AXES)
    row = P(DP, MP)
    return jax.shard_map(
        shards,
        mesh=fine,
        in_specs=(
            P(DP, None, None),
            P(DP),
            P(DP),
            P(),
            P(),
            row,
            row,
            row,
            P(MP, DP),
            row,
            row,
            P(None, None, MP),
        ),
        out_specs=(P(DP, None, None), P(DP, None, MP)),
        check_vma=False,
    )
```

```python
import functools

import jax
import jax.numpy as jnp
from jax import lax
from jax.experimental import pallas as pl
from jax.experimental.pallas import tpu as pltpu
from jax.sharding import Mesh, PartitionSpec as P

HD = 64
EPS = 1e-06
SCALE = 0.125
AXES = ("y", "xh", "z", "xl", "c")
NY, NXH, NZ, NXL, NC = 4, 2, 4, 2, 2
DP = ("y", "xh", "z")
MP = ("xl", "c")
SEQ = 128
PAIR = 2 * HD
HALVES = 2
VMEM = 52 * 1024 * 1024


def swap(values, axis):
    return lax.ppermute(values, axis, [(0, 1), (1, 0)])


RING = (0, 3, 1, 2)
OFFSETS = ((0, 0), (3, 0), (1, 0), (2, 0), (2, 2))


def shift(values, axis, by):
    size = lax.axis_size(axis)
    return lax.ppermute(values, axis, [(i, (i + by) % size) for i in range(size)])


def ring_gather(values, axis):
    return jnp.stack([values, shift(values, axis, 1), shift(values, axis, -1), shift(values, axis, 2)])


def ring_pieces(values, axis):
    below, above = shift(values, axis, 1), shift(values, axis, -1)
    half = values.shape[0] // 2
    return [values, below, above, shift(below[:half], axis, 1), shift(above[half:], axis, -1)]


def anywhere():
    return pl.BlockSpec(memory_space=pl.ANY)


def in_smem():
    return pl.BlockSpec(memory_space=pltpu.SMEM)


def load_weights(which, where_ref, gathered_ref, weight, sem_w):
    xh = where_ref[1]
    for y in range(NY):
        for j in range(NXH):
            xh_from = xh if j == 0 else 1 - xh
            pltpu.make_async_copy(
                gathered_ref.at[pl.ds(y * NZ, NZ), j, which],
                weight.at[which, pl.ds((y * NXH + xh_from) * NZ, NZ)],
                sem_w.at[which],
            ).start()


def attend_kernel(half, where_ref, lens_ref, normed_ref, weights_ref, out_ref, rows, weight, qkv, sem_a, sem_w):
    count, blocks, _, cols = weight.shape
    tokens = rows.shape[0]
    copy_rows = pltpu.make_async_copy(normed_ref.at[pl.ds(half * tokens, tokens)], rows, sem_a)
    copy_rows.start()
    load_weights(0, where_ref, weights_ref, weight, sem_w)
    copy_rows.wait()
    wide = 512
    for which in range(count):
        pltpu.make_async_copy(weight.at[which], weight.at[which], sem_w.at[which]).wait()
        if which + 1 < count:
            load_weights(which + 1, where_ref, weights_ref, weight, sem_w)

        def step(i, _, which=which):
            at = pl.multiple_of(i * wide, wide)
            acc = jnp.dot(
                rows[...],
                weight[which, :, :, pl.ds(at, wide)].reshape(blocks * SEQ, wide),
                preferred_element_type=jnp.float32,
            )
            qkv[which, :, pl.ds(at, wide)] = acc.astype(jnp.bfloat16)
            return 0

        lax.fori_loop(0, cols // wide, step, 0)

    lane = lax.broadcasted_iota(jnp.int32, (1, PAIR), 1)
    low = (lane < HD).astype(jnp.bfloat16)
    high = (lane >= HD).astype(jnp.bfloat16)

    def one(p, _):
        at = pl.multiple_of(p * SEQ, SEQ)
        seen = lane < lens_ref[half * (tokens // SEQ) + p]
        for hp in range(cols // PAIR):
            here = slice(hp * PAIR, (hp + 1) * PAIR)
            q = qkv[0, pl.ds(at, SEQ), here]
            k = qkv[1, pl.ds(at, SEQ), here]
            v = qkv[2, pl.ds(at, SEQ), here]
            q_two = jnp.concatenate([q * low, q * high], axis=0)
            scores = lax.dot_general(q_two, k, (((1,), (1,)), ((), ())), preferred_element_type=jnp.float32) * SCALE
            expon = jnp.where(seen, jnp.exp(scores), 0.0)
            share = (expon / jnp.sum(expon, axis=-1, keepdims=True)).astype(jnp.bfloat16)
            both = jnp.dot(share, v, preferred_element_type=jnp.float32)
            out_ref[pl.ds(at, SEQ), here] = jnp.where(lane < HD, both[:SEQ], both[SEQ:]).astype(jnp.bfloat16)
        return 0

    lax.fori_loop(0, tokens // SEQ, one, 0)


def attend(half, where, lengths, normed, gathered):
    total, width = normed.shape
    tokens = total // HALVES
    cols = gathered.shape[-1]
    return pl.pallas_call(
        functools.partial(attend_kernel, half),
        out_shape=jax.ShapeDtypeStruct((tokens, cols), jnp.bfloat16),
        in_specs=[in_smem(), in_smem(), anywhere(), anywhere()],
        out_specs=pl.BlockSpec(memory_space=pltpu.VMEM),
        scratch_shapes=[
            pltpu.VMEM((tokens, width), jnp.bfloat16),
            pltpu.VMEM((3, width // SEQ, SEQ, cols), jnp.bfloat16),
            pltpu.VMEM((3, tokens, cols), jnp.bfloat16),
            pltpu.SemaphoreType.DMA,
            pltpu.SemaphoreType.DMA((3,)),
        ],
        compiler_params=pltpu.CompilerParams(vmem_limit_bytes=VMEM),
        cost_estimate=pl.CostEstimate(flops=2 * tokens * width * cols * 3, bytes_accessed=18 << 20, transcendentals=tokens * SEQ * 8),
    )(where, lengths, normed, gathered)


def output_kernel(where_ref, mine_ref, other_ref, *rest):
    pieces, (out_ref, rows, weight, result, sem_a, sem_w, sem_o) = rest[: len(OFFSETS)], rest[len(OFFSETS) :]
    tokens, cols = mine_ref.shape
    y, xh, z, xl = (where_ref[i] for i in range(4))
    mine_at = pl.multiple_of(xl * cols, cols)
    other_at = pl.multiple_of((1 - xl) * cols, cols)
    pltpu.make_async_copy(mine_ref, rows.at[:, pl.ds(mine_at, cols)], sem_a).start()
    pltpu.make_async_copy(other_ref, rows.at[:, pl.ds(other_at, cols)], sem_a).start()
    part = weight.shape[2]

    def load_quarter(j):
        for piece, (dx, first) in zip(pieces, OFFSETS):
            x_from = lax.rem(xh * NXL + xl + dx, NXH * NXL)
            row = pl.multiple_of(lax.rem(x_from, NXL) * cols, cols)
            for i in range(piece.shape[0]):
                z_from = lax.rem(z + RING[first + i], NZ)
                at = pl.multiple_of(((x_from // NXL) * NZ + z_from) * SEQ, SEQ)
                pltpu.make_async_copy(
                    piece.at[i, j], weight.at[j, pl.ds(row, cols), pl.ds(at, SEQ)], sem_w.at[j]
                ).start()

    def store_quarter(j):
        y_from = lax.rem(y + RING[j], NY)
        return pltpu.make_async_copy(
            result.at[j], out_ref.at[:, pl.ds(pl.multiple_of(y_from * part, part), part)], sem_o.at[j]
        )

    load_quarter(0)
    load_quarter(1)
    pltpu.make_async_copy(rows, rows, sem_a).wait()
    wide = 512
    for j in range(NY):
        pltpu.make_async_copy(weight.at[j], weight.at[j], sem_w.at[j]).wait()
        if j + 2 < NY:
            load_quarter(j + 2)

        def step(i, _, j=j):
            at = pl.multiple_of(i * wide, wide)
            acc = jnp.dot(rows[...], weight[j, :, pl.ds(at, wide)], preferred_element_type=jnp.float32)
            result[j, :, pl.ds(at, wide)] = acc.astype(jnp.bfloat16)
            return 0

        lax.fori_loop(0, part // wide, step, 0)
        store_quarter(j).start()
    for j in range(NY):
        store_quarter(j).wait()


def output(where, mine, other, pieces, width):
    tokens, cols = mine.shape
    return pl.pallas_call(
        output_kernel,
        out_shape=jax.ShapeDtypeStruct((tokens, width), jnp.bfloat16),
        in_specs=[in_smem()] + [anywhere()] * (2 + len(pieces)),
        out_specs=anywhere(),
        scratch_shapes=[
            pltpu.VMEM((tokens, 2 * cols), jnp.bfloat16),
            pltpu.VMEM((NY, 2 * cols, width // NY), jnp.bfloat16),
            pltpu.VMEM((NY, tokens, width // NY), jnp.bfloat16),
            pltpu.SemaphoreType.DMA,
            pltpu.SemaphoreType.DMA((NY,)),
            pltpu.SemaphoreType.DMA((NY,)),
        ],
        compiler_params=pltpu.CompilerParams(vmem_limit_bytes=VMEM),
        cost_estimate=pl.CostEstimate(flops=4 * tokens * width * cols, bytes_accessed=13 << 20, transcendentals=0),
    )(where, mine, other, *pieces)


def encode_kernel(gain_ref, passages_ref, mine_ref, other_ref, *rest):
    encoded_ref, final_ref = rest[-2:]
    floats = passages_ref[...].astype(jnp.float32)
    summed = mine_ref[...].astype(jnp.float32) + other_ref[...].astype(jnp.float32)
    encoded = (floats + summed).astype(jnp.bfloat16)
    encoded_ref[...] = encoded
    values = encoded.astype(jnp.float32)
    mean = jnp.mean(values * values, axis=-1, keepdims=True)
    final_ref[...] = (values * lax.rsqrt(mean + EPS) * gain_ref[...]).astype(jnp.bfloat16)


def encode(half, gain, passages, mine, other, prior):
    tokens, width = mine.shape
    steps = tokens // SEQ
    block = (SEQ, width)
    in_specs = [
        pl.BlockSpec((1, width), lambda i: (0, 0)),
        pl.BlockSpec(block, lambda i: (half * steps + i, 0)),
        pl.BlockSpec(block, lambda i: (i, 0)),
        pl.BlockSpec(block, lambda i: (i, 0)),
    ]
    args = [gain, passages, mine, other]
    aliases = {}
    if prior is not None:
        in_specs += [anywhere()]
        args += [prior]
        aliases = {4: 0}
    return pl.pallas_call(
        encode_kernel,
        grid=(steps,),
        out_shape=(
            jax.ShapeDtypeStruct(passages.shape, jnp.bfloat16),
            jax.ShapeDtypeStruct((tokens, width), jnp.bfloat16),
        ),
        in_specs=in_specs,
        out_specs=(pl.BlockSpec(block, lambda i: (half * steps + i, 0)), pl.BlockSpec(block, lambda i: (i, 0))),
        input_output_aliases=aliases,
        compiler_params=pltpu.CompilerParams(vmem_limit_bytes=32 * 1024 * 1024),
        cost_estimate=pl.CostEstimate(flops=8 * tokens * width, bytes_accessed=20 << 20, transcendentals=0),
    )(*args)


def decode_kernel(where_ref, lens_ref, owner_ref, query_ref, *rest):
    finals, rest = rest[:HALVES], rest[HALVES:]
    weights_ref, sent_ref, final, weight, kv, numer, sem_a, sem_w = rest
    count, blocks, _, cols = weight.shape
    tokens = final.shape[1]
    pltpu.make_async_copy(finals[0], final.at[0], sem_a.at[0]).start()
    load_weights(0, where_ref, weights_ref, weight, sem_w)
    numer[...] = jnp.zeros_like(numer)

    lane = lax.broadcasted_iota(jnp.int32, (1, PAIR), 1)
    low = (lane < HD).astype(jnp.bfloat16)
    high = (lane >= HD).astype(jnp.bfloat16)
    dec_len = query_ref.shape[1]
    wide = 512
    for half in range(HALVES):
        pltpu.make_async_copy(final.at[half], final.at[half], sem_a.at[half]).wait()
        for which in range(count):
            if half == 0:
                pltpu.make_async_copy(weight.at[which], weight.at[which], sem_w.at[which]).wait()
                if which == 0:
                    load_weights(1, where_ref, weights_ref, weight, sem_w)
                else:
                    pltpu.make_async_copy(finals[1], final.at[1], sem_a.at[1]).start()

            def column(i, _, which=which, half=half):
                at = pl.multiple_of(i * wide, wide)
                acc = jnp.dot(
                    final[half],
                    weight[which, :, :, pl.ds(at, wide)].reshape(blocks * SEQ, wide),
                    preferred_element_type=jnp.float32,
                )
                kv[which, :, pl.ds(at, wide)] = acc.astype(jnp.bfloat16)
                return 0

            lax.fori_loop(0, cols // wide, column, 0)

        def one(p, _, half=half):
            at = pl.multiple_of(p * SEQ, SEQ)
            seen = lane < lens_ref[half * (tokens // SEQ) + p]
            question = owner_ref[half * (tokens // SEQ) + p]
            totals = jnp.zeros((dec_len, PAIR), jnp.float32)
            for hp in range(cols // PAIR):
                here = slice(hp * PAIR, (hp + 1) * PAIR)
                q = query_ref[question, :, here]
                k = kv[0, pl.ds(at, SEQ), here]
                v = kv[1, pl.ds(at, SEQ), here]
                q_two = jnp.concatenate([q * low, q * high], axis=0)
                scores = lax.dot_general(q_two, k, (((1,), (1,)), ((), ())), preferred_element_type=jnp.float32) * SCALE
                expon = jnp.where(seen, jnp.exp(scores), 0.0)
                total = jnp.sum(expon, axis=-1, keepdims=True)
                coarse = expon.astype(jnp.bfloat16)
                fine = (expon - coarse.astype(jnp.float32)).astype(jnp.bfloat16)
                both = jnp.dot(coarse, v, preferred_element_type=jnp.float32) + jnp.dot(
                    fine, v, preferred_element_type=jnp.float32
                )
                rows = slice(hp * dec_len, (hp + 1) * dec_len)
                numer[question, rows, :] += jnp.where(lane < HD, both[:dec_len], both[dec_len:])
                totals = jnp.where(lane == 2 * hp, total[:dec_len], totals)
                totals = jnp.where(lane == 2 * hp + 1, total[dec_len:], totals)
            packed = totals[:8]
            for group in range(1, dec_len // 8):
                packed += pltpu.roll(totals[8 * group : 8 * (group + 1)], 8 * group, 1)
            numer[question, cols // PAIR * dec_len : cols // PAIR * dec_len + 8, :] += packed
            return 0

        lax.fori_loop(0, tokens // SEQ, one, 0)
    sent_ref[...] = numer[...].astype(jnp.bfloat16)


def decode(where, lengths, owner, query, finals, gathered):
    tokens, width = finals[0].shape
    questions, dec_len, cols = query.shape
    shape = (questions, cols // PAIR * dec_len + 16, PAIR)
    return pl.pallas_call(
        decode_kernel,
        out_shape=jax.ShapeDtypeStruct(shape, jnp.bfloat16),
        in_specs=[in_smem()] * 3 + [pl.BlockSpec(memory_space=pltpu.VMEM)] + [anywhere()] * (HALVES + 1),
        out_specs=pl.BlockSpec(memory_space=pltpu.VMEM),
        scratch_shapes=[
            pltpu.VMEM((HALVES, tokens, width), jnp.bfloat16),
            pltpu.VMEM((2, width // SEQ, SEQ, cols), jnp.bfloat16),
            pltpu.VMEM((2, tokens, cols), jnp.bfloat16),
            pltpu.VMEM(shape, jnp.float32),
            pltpu.SemaphoreType.DMA((HALVES,)),
            pltpu.SemaphoreType.DMA((2,)),
        ],
        compiler_params=pltpu.CompilerParams(vmem_limit_bytes=VMEM),
        cost_estimate=pl.CostEstimate(
            flops=4 * HALVES * tokens * width * cols, bytes_accessed=18 << 20, transcendentals=1 << 18
        ),
    )(where, lengths, owner, query, *finals, gathered)


def gather_rows(mine, other):
    both = jnp.stack([mine, other])
    return lax.all_gather(both, ("y", "z"), axis=0, tiled=False).reshape((NY * NZ,) + both.shape)


def shards(
    passages,
    lengths,
    owner,
    enc_gain,
    final_gain,
    enc_wq,
    enc_wk,
    enc_wv,
    enc_wo,
    dec_wk,
    dec_wv,
    dec_query,
):
    pass_count, seq_len, width = passages.shape
    tok_rows = pass_count * seq_len
    local_cols = enc_wq.shape[1]
    local_heads = local_cols // HD
    dec_len = dec_query.shape[1]
    flat = passages.reshape(tok_rows, width)
    floats = flat.astype(jnp.float32)
    mean = jnp.mean(floats * floats, axis=-1, keepdims=True)
    normed = (floats * lax.rsqrt(mean + EPS) * enc_gain).astype(jnp.bfloat16)

    enc = jnp.stack([enc_wq, enc_wk, enc_wv])
    enc_other = swap(enc, "xh")
    wo = ring_gather(enc_wo, "y")
    enc, enc_other, wo = lax.optimization_barrier((enc, enc_other, wo))
    qkv = gather_rows(enc, enc_other)
    *wo, low, high = ring_pieces(wo, "z")
    wo = jnp.stack([*wo, jnp.concatenate([low, high])])
    dec, wo = lax.optimization_barrier((jnp.stack([dec_wk, dec_wv]), wo))
    dkv = gather_rows(dec, swap(dec, "xh"))
    wo = ring_pieces(wo, ("xh", "xl"))
    where = jnp.stack([lax.axis_index(axis) for axis in AXES]).astype(jnp.int32)
    mine = [attend(half, where, lengths, normed, qkv) for half in range(HALVES)]
    theirs = [swap(part, "xl") for part in mine]
    partial = [output(where, mine[half], theirs[half], wo, width) for half in range(HALVES)]
    partial_other = [swap(part, "c") for part in partial]
    encoded = None
    finals = []
    for half in range(HALVES):
        encoded, final = encode(half, final_gain.reshape(1, width), flat, partial[half], partial_other[half], encoded)
        finals.append(final)
    sent = decode(where, lengths, owner, dec_query, finals, dkv)
    came = lax.all_to_all(sent, DP, 0, 0, tiled=True).astype(jnp.float32)
    came = jnp.sum(came, axis=0)
    pairs = local_heads // 2
    own_numer = came[: pairs * dec_len].reshape(pairs, dec_len, 2, HD).transpose(1, 0, 2, 3)
    own_total = came[pairs * dec_len : pairs * dec_len + 8, : dec_len // 8 * local_heads]
    own_total = own_total.reshape(8, dec_len // 8, local_heads).transpose(1, 0, 2).reshape(dec_len, pairs, 2, 1)
    context = (own_numer / own_total).astype(jnp.bfloat16).reshape(1, dec_len, local_cols)
    return (encoded.reshape(pass_count, seq_len, width), context)


def solution(mesh):
    fine = Mesh(mesh.devices.reshape((NY, NXH, NZ, NXL, NC)), AXES)
    row = P(DP, MP)
    return jax.shard_map(
        shards,
        mesh=fine,
        in_specs=(
            P(DP, None, None),
            P(DP),
            P(DP),
            P(),
            P(),
            row,
            row,
            row,
            P(MP, DP),
            row,
            row,
            P(None, None, MP),
        ),
        out_specs=(P(DP, None, None), P(DP, None, MP)),
        check_vma=False,
    )
```

```python
import functools

import jax
import jax.numpy as jnp
from jax import lax
from jax.experimental import pallas as pl
from jax.experimental.pallas import tpu as pltpu
from jax.sharding import Mesh, PartitionSpec as P

HD = 64
EPS = 1e-06
SCALE = 0.125
AXES = ("y", "xh", "z", "xl", "c")
NY, NXH, NZ, NXL, NC = 4, 2, 4, 2, 2
DP = ("y", "xh", "z")
MP = ("xl", "c")
SEQ = 128
PAIR = 2 * HD
HALVES = 2
VMEM = 52 * 1024 * 1024


def swap(values, axis):
    return lax.ppermute(values, axis, [(0, 1), (1, 0)])


RING = (0, 3, 1, 2)
OFFSETS = ((0, 0), (3, 0), (1, 0), (2, 0), (2, 2))


def shift(values, axis, by):
    size = lax.axis_size(axis)
    return lax.ppermute(values, axis, [(i, (i + by) % size) for i in range(size)])


def ring_gather(values, axis):
    return jnp.stack([values, shift(values, axis, 1), shift(values, axis, -1), shift(values, axis, 2)])


def ring_pieces(values, axis):
    below, above = shift(values, axis, 1), shift(values, axis, -1)
    half = values.shape[0] // 2
    return [values, below, above, shift(below[:half], axis, 1), shift(above[half:], axis, -1)]


def anywhere():
    return pl.BlockSpec(memory_space=pl.ANY)


def in_smem():
    return pl.BlockSpec(memory_space=pltpu.SMEM)


def load_weights(which, where_ref, gathered_ref, weight, sem_w):
    xh = where_ref[1]
    for y in range(NY):
        for j in range(NXH):
            xh_from = xh if j == 0 else 1 - xh
            pltpu.make_async_copy(
                gathered_ref.at[pl.ds(y * NZ, NZ), j, which],
                weight.at[which, pl.ds((y * NXH + xh_from) * NZ, NZ)],
                sem_w.at[which],
            ).start()


def attend_kernel(half, where_ref, lens_ref, normed_ref, weights_ref, out_ref, rows, weight, qkv, sem_a, sem_w):
    count, blocks, _, cols = weight.shape
    tokens = rows.shape[0]
    copy_rows = pltpu.make_async_copy(normed_ref.at[pl.ds(half * tokens, tokens)], rows, sem_a)
    copy_rows.start()
    load_weights(0, where_ref, weights_ref, weight, sem_w)
    copy_rows.wait()
    wide = 512
    for which in range(count):
        pltpu.make_async_copy(weight.at[which], weight.at[which], sem_w.at[which]).wait()
        if which + 1 < count:
            load_weights(which + 1, where_ref, weights_ref, weight, sem_w)

        def step(i, _, which=which):
            at = pl.multiple_of(i * wide, wide)
            acc = jnp.dot(
                rows[...],
                weight[which, :, :, pl.ds(at, wide)].reshape(blocks * SEQ, wide),
                preferred_element_type=jnp.float32,
            )
            qkv[which, :, pl.ds(at, wide)] = acc.astype(jnp.bfloat16)
            return 0

        lax.fori_loop(0, cols // wide, step, 0)

    lane = lax.broadcasted_iota(jnp.int32, (1, PAIR), 1)
    low = (lane < HD).astype(jnp.bfloat16)
    high = (lane >= HD).astype(jnp.bfloat16)

    def one(p, _):
        at = pl.multiple_of(p * SEQ, SEQ)
        seen = lane < lens_ref[half * (tokens // SEQ) + p]
        for hp in range(cols // PAIR):
            here = slice(hp * PAIR, (hp + 1) * PAIR)
            q = qkv[0, pl.ds(at, SEQ), here]
            k = qkv[1, pl.ds(at, SEQ), here]
            v = qkv[2, pl.ds(at, SEQ), here]
            q_two = jnp.concatenate([q * low, q * high], axis=0)
            scores = lax.dot_general(q_two, k, (((1,), (1,)), ((), ())), preferred_element_type=jnp.float32) * SCALE
            expon = jnp.where(seen, jnp.exp(scores), 0.0)
            share = (expon / jnp.sum(expon, axis=-1, keepdims=True)).astype(jnp.bfloat16)
            both = jnp.dot(share, v, preferred_element_type=jnp.float32)
            out_ref[pl.ds(at, SEQ), here] = jnp.where(lane < HD, both[:SEQ], both[SEQ:]).astype(jnp.bfloat16)
        return 0

    lax.fori_loop(0, tokens // SEQ, one, 0)


def attend(half, where, lengths, normed, gathered):
    total, width = normed.shape
    tokens = total // HALVES
    cols = gathered.shape[-1]
    return pl.pallas_call(
        functools.partial(attend_kernel, half),
        out_shape=jax.ShapeDtypeStruct((tokens, cols), jnp.bfloat16),
        in_specs=[in_smem(), in_smem(), anywhere(), anywhere()],
        out_specs=pl.BlockSpec(memory_space=pltpu.VMEM),
        scratch_shapes=[
            pltpu.VMEM((tokens, width), jnp.bfloat16),
            pltpu.VMEM((3, width // SEQ, SEQ, cols), jnp.bfloat16),
            pltpu.VMEM((3, tokens, cols), jnp.bfloat16),
            pltpu.SemaphoreType.DMA,
            pltpu.SemaphoreType.DMA((3,)),
        ],
        compiler_params=pltpu.CompilerParams(vmem_limit_bytes=VMEM),
        cost_estimate=pl.CostEstimate(flops=2 * tokens * width * cols * 3, bytes_accessed=18 << 20, transcendentals=tokens * SEQ * 8),
    )(where, lengths, normed, gathered)


def output_kernel(where_ref, mine_ref, other_ref, *rest):
    pieces, (out_ref, rows, weight, result, sem_a, sem_w, sem_o) = rest[: len(OFFSETS)], rest[len(OFFSETS) :]
    tokens, cols = mine_ref.shape
    y, xh, z, xl = (where_ref[i] for i in range(4))
    mine_at = pl.multiple_of(xl * cols, cols)
    other_at = pl.multiple_of((1 - xl) * cols, cols)
    pltpu.make_async_copy(mine_ref, rows.at[:, pl.ds(mine_at, cols)], sem_a).start()
    pltpu.make_async_copy(other_ref, rows.at[:, pl.ds(other_at, cols)], sem_a).start()
    part = weight.shape[2]

    def load_quarter(j):
        for piece, (dx, first) in zip(pieces, OFFSETS):
            x_from = lax.rem(xh * NXL + xl + dx, NXH * NXL)
            row = pl.multiple_of(lax.rem(x_from, NXL) * cols, cols)
            for i in range(piece.shape[0]):
                z_from = lax.rem(z + RING[first + i], NZ)
                at = pl.multiple_of(((x_from // NXL) * NZ + z_from) * SEQ, SEQ)
                pltpu.make_async_copy(
                    piece.at[i, j], weight.at[j, pl.ds(row, cols), pl.ds(at, SEQ)], sem_w.at[j]
                ).start()

    def store_quarter(j):
        y_from = lax.rem(y + RING[j], NY)
        return pltpu.make_async_copy(
            result.at[j], out_ref.at[:, pl.ds(pl.multiple_of(y_from * part, part), part)], sem_o.at[j]
        )

    load_quarter(0)
    load_quarter(1)
    pltpu.make_async_copy(rows, rows, sem_a).wait()
    wide = 512
    for j in range(NY):
        pltpu.make_async_copy(weight.at[j], weight.at[j], sem_w.at[j]).wait()
        if j + 2 < NY:
            load_quarter(j + 2)

        def step(i, _, j=j):
            at = pl.multiple_of(i * wide, wide)
            acc = jnp.dot(rows[...], weight[j, :, pl.ds(at, wide)], preferred_element_type=jnp.float32)
            result[j, :, pl.ds(at, wide)] = acc.astype(jnp.bfloat16)
            return 0

        lax.fori_loop(0, part // wide, step, 0)
        store_quarter(j).start()
    for j in range(NY):
        store_quarter(j).wait()


def output(where, mine, other, pieces, width):
    tokens, cols = mine.shape
    return pl.pallas_call(
        output_kernel,
        out_shape=jax.ShapeDtypeStruct((tokens, width), jnp.bfloat16),
        in_specs=[in_smem()] + [anywhere()] * (2 + len(pieces)),
        out_specs=anywhere(),
        scratch_shapes=[
            pltpu.VMEM((tokens, 2 * cols), jnp.bfloat16),
            pltpu.VMEM((NY, 2 * cols, width // NY), jnp.bfloat16),
            pltpu.VMEM((NY, tokens, width // NY), jnp.bfloat16),
            pltpu.SemaphoreType.DMA,
            pltpu.SemaphoreType.DMA((NY,)),
            pltpu.SemaphoreType.DMA((NY,)),
        ],
        compiler_params=pltpu.CompilerParams(vmem_limit_bytes=VMEM),
        cost_estimate=pl.CostEstimate(flops=4 * tokens * width * cols, bytes_accessed=13 << 20, transcendentals=0),
    )(where, mine, other, *pieces)


def encode_kernel(gain_ref, passages_ref, mine_ref, other_ref, *rest):
    encoded_ref, final_ref = rest[-2:]
    floats = passages_ref[...].astype(jnp.float32)
    summed = mine_ref[...].astype(jnp.float32) + other_ref[...].astype(jnp.float32)
    encoded = (floats + summed).astype(jnp.bfloat16)
    encoded_ref[...] = encoded
    values = encoded.astype(jnp.float32)
    mean = jnp.mean(values * values, axis=-1, keepdims=True)
    final_ref[...] = (values * lax.rsqrt(mean + EPS) * gain_ref[...]).astype(jnp.bfloat16)


def encode(half, gain, passages, mine, other, prior):
    tokens, width = mine.shape
    steps = tokens // SEQ
    block = (SEQ, width)
    in_specs = [
        pl.BlockSpec((1, width), lambda i: (0, 0)),
        pl.BlockSpec(block, lambda i: (half * steps + i, 0)),
        pl.BlockSpec(block, lambda i: (i, 0)),
        pl.BlockSpec(block, lambda i: (i, 0)),
    ]
    args = [gain, passages, mine, other]
    aliases = {}
    if prior is not None:
        in_specs += [anywhere()]
        args += [prior]
        aliases = {4: 0}
    return pl.pallas_call(
        encode_kernel,
        grid=(steps,),
        out_shape=(
            jax.ShapeDtypeStruct(passages.shape, jnp.bfloat16),
            jax.ShapeDtypeStruct((tokens, width), jnp.bfloat16),
        ),
        in_specs=in_specs,
        out_specs=(pl.BlockSpec(block, lambda i: (half * steps + i, 0)), pl.BlockSpec(block, lambda i: (i, 0))),
        input_output_aliases=aliases,
        compiler_params=pltpu.CompilerParams(vmem_limit_bytes=32 * 1024 * 1024),
        cost_estimate=pl.CostEstimate(flops=8 * tokens * width, bytes_accessed=20 << 20, transcendentals=0),
    )(*args)


def decode_kernel(where_ref, lens_ref, owner_ref, query_ref, *rest):
    finals, rest = rest[:HALVES], rest[HALVES:]
    weights_ref, sent_ref, final, weight, kv, numer, sem_a, sem_w = rest
    count, blocks, _, cols = weight.shape
    tokens = final.shape[1]
    pltpu.make_async_copy(finals[0], final.at[0], sem_a.at[0]).start()
    load_weights(0, where_ref, weights_ref, weight, sem_w)
    numer[...] = jnp.zeros_like(numer)

    lane = lax.broadcasted_iota(jnp.int32, (1, PAIR), 1)
    low = (lane < HD).astype(jnp.bfloat16)
    high = (lane >= HD).astype(jnp.bfloat16)
    dec_len = query_ref.shape[1]
    wide = 512
    for half in range(HALVES):
        pltpu.make_async_copy(final.at[half], final.at[half], sem_a.at[half]).wait()
        for which in range(count):
            if half == 0:
                pltpu.make_async_copy(weight.at[which], weight.at[which], sem_w.at[which]).wait()
                if which == 0:
                    load_weights(1, where_ref, weights_ref, weight, sem_w)
                else:
                    pltpu.make_async_copy(finals[1], final.at[1], sem_a.at[1]).start()

            def column(i, _, which=which, half=half):
                at = pl.multiple_of(i * wide, wide)
                acc = jnp.dot(
                    final[half],
                    weight[which, :, :, pl.ds(at, wide)].reshape(blocks * SEQ, wide),
                    preferred_element_type=jnp.float32,
                )
                kv[which, :, pl.ds(at, wide)] = acc.astype(jnp.bfloat16)
                return 0

            lax.fori_loop(0, cols // wide, column, 0)

        def one(p, _, half=half):
            at = pl.multiple_of(p * SEQ, SEQ)
            seen = lane < lens_ref[half * (tokens // SEQ) + p]
            question = owner_ref[half * (tokens // SEQ) + p]
            totals = jnp.zeros((dec_len, PAIR), jnp.float32)
            for hp in range(cols // PAIR):
                here = slice(hp * PAIR, (hp + 1) * PAIR)
                q = query_ref[question, :, here]
                k = kv[0, pl.ds(at, SEQ), here]
                v = kv[1, pl.ds(at, SEQ), here]
                q_two = jnp.concatenate([q * low, q * high], axis=0)
                scores = lax.dot_general(q_two, k, (((1,), (1,)), ((), ())), preferred_element_type=jnp.float32) * SCALE
                expon = jnp.where(seen, jnp.exp(scores), 0.0)
                total = jnp.sum(expon, axis=-1, keepdims=True)
                coarse = expon.astype(jnp.bfloat16)
                fine = (expon - coarse.astype(jnp.float32)).astype(jnp.bfloat16)
                both = jnp.dot(jnp.concatenate([coarse, fine], axis=0), v, preferred_element_type=jnp.float32)
                both = both[: 2 * dec_len] + both[2 * dec_len :]
                rows = slice(hp * dec_len, (hp + 1) * dec_len)
                numer[question, rows, :] += jnp.where(lane < HD, both[:dec_len], both[dec_len:])
                totals = jnp.where(lane == 2 * hp, total[:dec_len], totals)
                totals = jnp.where(lane == 2 * hp + 1, total[dec_len:], totals)
            packed = totals[:8]
            for group in range(1, dec_len // 8):
                packed += pltpu.roll(totals[8 * group : 8 * (group + 1)], 8 * group, 1)
            numer[question, cols // PAIR * dec_len : cols // PAIR * dec_len + 8, :] += packed
            return 0

        lax.fori_loop(0, tokens // SEQ, one, 0)
    sent_ref[...] = numer[...].astype(jnp.bfloat16)


def decode(where, lengths, owner, query, finals, gathered):
    tokens, width = finals[0].shape
    questions, dec_len, cols = query.shape
    shape = (questions, cols // PAIR * dec_len + 16, PAIR)
    return pl.pallas_call(
        decode_kernel,
        out_shape=jax.ShapeDtypeStruct(shape, jnp.bfloat16),
        in_specs=[in_smem()] * 3 + [pl.BlockSpec(memory_space=pltpu.VMEM)] + [anywhere()] * (HALVES + 1),
        out_specs=pl.BlockSpec(memory_space=pltpu.VMEM),
        scratch_shapes=[
            pltpu.VMEM((HALVES, tokens, width), jnp.bfloat16),
            pltpu.VMEM((2, width // SEQ, SEQ, cols), jnp.bfloat16),
            pltpu.VMEM((2, tokens, cols), jnp.bfloat16),
            pltpu.VMEM(shape, jnp.float32),
            pltpu.SemaphoreType.DMA((HALVES,)),
            pltpu.SemaphoreType.DMA((2,)),
        ],
        compiler_params=pltpu.CompilerParams(vmem_limit_bytes=VMEM),
        cost_estimate=pl.CostEstimate(
            flops=4 * HALVES * tokens * width * cols, bytes_accessed=18 << 20, transcendentals=1 << 18
        ),
    )(where, lengths, owner, query, *finals, gathered)


def gather_rows(mine, other):
    both = jnp.stack([mine, other])
    return lax.all_gather(both, ("y", "z"), axis=0, tiled=False).reshape((NY * NZ,) + both.shape)


def shards(
    passages,
    lengths,
    owner,
    enc_gain,
    final_gain,
    enc_wq,
    enc_wk,
    enc_wv,
    enc_wo,
    dec_wk,
    dec_wv,
    dec_query,
):
    pass_count, seq_len, width = passages.shape
    tok_rows = pass_count * seq_len
    local_cols = enc_wq.shape[1]
    local_heads = local_cols // HD
    dec_len = dec_query.shape[1]
    flat = passages.reshape(tok_rows, width)
    floats = flat.astype(jnp.float32)
    mean = jnp.mean(floats * floats, axis=-1, keepdims=True)
    normed = (floats * lax.rsqrt(mean + EPS) * enc_gain).astype(jnp.bfloat16)

    enc = jnp.stack([enc_wq, enc_wk, enc_wv])
    enc_other = swap(enc, "xh")
    wo = ring_gather(enc_wo, "y")
    enc, enc_other, wo = lax.optimization_barrier((enc, enc_other, wo))
    qkv = gather_rows(enc, enc_other)
    *wo, low, high = ring_pieces(wo, "z")
    wo = jnp.stack([*wo, jnp.concatenate([low, high])])
    dec, wo = lax.optimization_barrier((jnp.stack([dec_wk, dec_wv]), wo))
    dkv = gather_rows(dec, swap(dec, "xh"))
    wo = ring_pieces(wo, ("xh", "xl"))
    where = jnp.stack([lax.axis_index(axis) for axis in AXES]).astype(jnp.int32)
    mine = [attend(half, where, lengths, normed, qkv) for half in range(HALVES)]
    theirs = [swap(part, "xl") for part in mine]
    partial = [output(where, mine[half], theirs[half], wo, width) for half in range(HALVES)]
    partial_other = [swap(part, "c") for part in partial]
    encoded = None
    finals = []
    for half in range(HALVES):
        encoded, final = encode(half, final_gain.reshape(1, width), flat, partial[half], partial_other[half], encoded)
        finals.append(final)
    sent = decode(where, lengths, owner, dec_query, finals, dkv)
    came = lax.all_to_all(sent, DP, 0, 0, tiled=True).astype(jnp.float32)
    came = jnp.sum(came, axis=0)
    pairs = local_heads // 2
    own_numer = came[: pairs * dec_len].reshape(pairs, dec_len, 2, HD).transpose(1, 0, 2, 3)
    own_total = came[pairs * dec_len : pairs * dec_len + 8, : dec_len // 8 * local_heads]
    own_total = own_total.reshape(8, dec_len // 8, local_heads).transpose(1, 0, 2).reshape(dec_len, pairs, 2, 1)
    context = (own_numer / own_total).astype(jnp.bfloat16).reshape(1, dec_len, local_cols)
    return (encoded.reshape(pass_count, seq_len, width), context)


def solution(mesh):
    fine = Mesh(mesh.devices.reshape((NY, NXH, NZ, NXL, NC)), AXES)
    row = P(DP, MP)
    return jax.shard_map(
        shards,
        mesh=fine,
        in_specs=(
            P(DP, None, None),
            P(DP),
            P(DP),
            P(),
            P(),
            row,
            row,
            row,
            P(MP, DP),
            row,
            row,
            P(None, None, MP),
        ),
        out_specs=(P(DP, None, None), P(DP, None, MP)),
        check_vma=False,
    )
```
